128 devices in a mesh: dp: 16 (over y, x), tensor: 8 (over z, core).
Axes of the slice: x: 4, y: 4, z: 4, core: 2. Of those that a mesh axis runs over, the one named last changes fastest.
Arguments:
- hidden_acts: bfloat16 [16384, 12800], P('dp', 'tensor'), may hold values from -6 to 6
- out_grads: bfloat16 [16384, 2560], P(('dp', 'tensor')), may hold values from -0.1875 to 0.1875
- error: bfloat16 [16, 12800, 2560], P('dp', 'tensor'), may hold values from -6 to 6
- basis: bfloat16 [2560, 64], replicated, may hold values from -0.125 to 0.125
Outputs:
- update: bfloat16 [12800, 2560], P('tensor', 'dp')
- new_error: bfloat16 [16, 12800, 2560], P('dp', 'tensor')
The draws below stay inside these ranges and needn't reach their ends.
All inputs are finite; a program needn't handle non-finite values.
Results may differ from the reference program's by a relative error of at most 0.013.
Values may be sent and summed in bfloat16 or wider, within the bound.
A program may use at most 128 MiB of HBM per device.

```python
import jax
import jax.numpy as jnp
from jax import lax

FF = 12800
D = 2560
R = 64
TOK_DEV = 1024
TOKENS = 16384
N_DP = 16


def level_of(stream_key, shape, cuts, low, high):
    gain, own = 1.0, jax.random.fold_in(stream_key, 6)
    for dim, shards_of in cuts:
        heights = jnp.exp(jax.random.uniform(jax.random.fold_in(own, dim), (shards_of,), jnp.float32, low / len(cuts), high / len(cuts)))
        gain = gain * jnp.repeat(heights, shape[dim] // shards_of).reshape([-1 if axis == dim else 1 for axis in range(len(shape))])
    return gain


def centred(key, extent, spread, most, split=(), held_as=jnp.bfloat16):
    result = spread * jax.random.normal(key, extent, jnp.float32)
    if split:
        result = result * level_of(key, extent, split, -0.22, 0.18)
    return jnp.clip(result, -most, most).astype(held_as)


def setup_inputs(seed: int = 0) -> dict:
    splits = jax.random.split(jax.random.key(seed), 5)
    hidden_acts = centred(splits[0], (TOKENS, FF), 1.0, 6.0, ((0, 16), (1, 8)))
    out_grads = centred(splits[1], (TOKENS, D), TOK_DEV ** -0.5, 0.1875, ((0, 128),))
    error = centred(splits[2], (N_DP, FF, D), 1.0, 6.0, ((0, 16), (1, 8)))
    basis = centred(splits[3], (D, R), D ** -0.5, 0.125)
    return {"hidden_acts": hidden_acts, "out_grads": out_grads, "error": error, "basis": basis}


def reference(hidden_acts, out_grads, error, basis):
    acts = hidden_acts.reshape(N_DP, TOK_DEV, FF)
    grads = out_grads.reshape(N_DP, TOK_DEV, D)

    def form(items):
        act_block, grad_block, err_block = items
        grad = lax.dot_general(act_block.astype(jnp.float32), grad_block.astype(jnp.float32), (((0,), (0,)), ((), ())), preferred_element_type=jnp.float32)
        return (grad + err_block.astype(jnp.float32)).astype(jnp.bfloat16)
    merged = lax.map(form, (acts, grads, error))

    def left_term(carry, block):
        return (carry + jnp.dot(block.astype(jnp.float32), basis.astype(jnp.float32), preferred_element_type=jnp.float32), None)
    p_sum, _ = lax.scan(left_term, jnp.zeros((FF, R), jnp.float32), merged)
    gram = jnp.dot(p_sum.T, p_sum, precision=lax.Precision.HIGHEST)
    lower = jnp.linalg.cholesky(gram)
    solved = jax.scipy.linalg.solve_triangular(lower, p_sum.T, lower=True)
    p_hat = solved.T.astype(jnp.bfloat16)

    def right_term(carry, block):
        term = lax.dot_general(block.astype(jnp.float32), p_hat.astype(jnp.float32), (((0,), (0,)), ((), ())), preferred_element_type=jnp.float32)
        return (carry + term, None)
    q_sum, _ = lax.scan(right_term, jnp.zeros((D, R), jnp.float32), merged)
    full = jnp.dot(p_hat.astype(jnp.float32), q_sum.T, precision=lax.Precision.HIGHEST) / N_DP
    update = full.astype(jnp.bfloat16)
    new_error = lax.map(lambda block: (block.astype(jnp.float32) - full).astype(jnp.bfloat16), merged)
    return (update, new_error)
```

```python
import functools

import jax
import jax.numpy as jnp
from jax import lax
from jax.experimental import pallas as pl
from jax.experimental.pallas import tpu as pltpu
from jax.sharding import PartitionSpec as P

MESH = pl.DeviceIdType.MESH
F32 = jnp.float32
BF16 = jnp.bfloat16
CHUNK = 256
FILL = {"left_sum": 1, "left_rows": 2, "gram": 2, "right_sum": 3, "right_cross": 2}


def mm(a, b):
    return lax.dot_general(a, b, (((1,), (0,)), ((), ())), preferred_element_type=F32)


def mm_tn(a, b):
    return lax.dot_general(a, b, (((0,), (0,)), ((), ())), preferred_element_type=F32)


def mm_nt(a, b):
    return lax.dot_general(a, b, (((1,), (1,)), ((), ())), preferred_element_type=F32)


def fold(x):
    return x + pltpu.roll(x, x.shape[1] // 2, 1)


def pair(x):
    lane = lax.broadcasted_iota(jnp.int32, x.shape, 1)
    high = x.astype(BF16).astype(F32)
    return jnp.where(lane < x.shape[1] // 2, x, x - high).astype(BF16)


def split_of(n_dp):
    rows = 1
    while rows * rows < n_dp:
        rows *= 2
    return rows, n_dp // rows


def rows_step(total):
    for step in (320, 160, 80, 64, 32, 16):
        if total % step == 0:
            return step
    return total


def step_kernel(
    n_dp, n_t,
    a_hbm, g_hbm, e_hbm, b_hbm,
    merged_hbm, phat_out, qt_out,
    a_ref, at_ref, e_ref, g_own, g_all, basis_ref, bb_ref, merged_ref,
    gb_all, ep_ref, p_send, p_parts, p_all, gram_all, elim_ref,
    pt_ref, y_send, y_parts, q_loc, q_send, q_parts, q_cross,
    load_sem, loc_sem, out_sem, ag_send, ag_recv,
    x1s, x1r, x2s, x2r, x3s, x3r, x4s, x4r, x5s, x5r, x6s, x6r, x7s, x7r, x8s, x8r,
):
    toks, ffl = a_ref.shape
    own_toks, d_model = g_own.shape
    n_chunk = g_all.shape[0]
    width = g_all.shape[2]
    rank = qt_out.shape[0]
    half = own_toks // 2
    part = p_parts.shape[1]
    q_rows, q_cols = q_parts.shape[1:]
    q_split = d_model // q_cols
    d = lax.axis_index("dp")
    t = lax.axis_index("tensor")
    core = lax.rem(t, 2)
    partner = t + 1 - 2 * core
    up = lax.rem(t + 2, n_t)
    down = lax.rem(t + n_t - 2, n_t)
    across = lax.rem(t + 4, n_t)

    def other(block):
        return block + 1 - 2 * lax.rem(block, 2)

    step = rows_step(ffl)
    n_step = ffl // step
    load_g = pltpu.make_async_copy(g_hbm, g_own, load_sem.at[0])
    load_b = pltpu.make_async_copy(b_hbm, basis_ref, load_sem.at[1])
    load_a = pltpu.make_async_copy(a_hbm, a_ref, load_sem.at[2])
    load_g.start()
    load_b.start()

    def load_e(i):
        rows = pl.ds(pl.multiple_of(i * step, step), step)
        return pltpu.make_async_copy(e_hbm.at[0, rows, :], e_ref.at[rows, :], load_sem.at[3 + i])

    for i in range(n_step):
        load_e(i).start()
    load_a.start()

    barrier = pltpu.get_barrier_semaphore()

    def greet_t(k, _):
        pl.semaphore_signal(barrier, inc=1, device_id=(d, lax.rem(t + k, n_t)), device_id_type=MESH)
        return 0

    def greet_d(k, _):
        pl.semaphore_signal(barrier, inc=1, device_id=(lax.rem(d + k, n_dp), t), device_id_type=MESH)
        return 0

    lax.fori_loop(1, n_t, greet_t, 0)
    lax.fori_loop(1, n_dp, greet_d, 0)

    def remote(src, dst, ssem, rsem, dev):
        return pltpu.make_async_remote_copy(
            src_ref=src, dst_ref=dst, send_sem=ssem, recv_sem=rsem, device_id=dev, device_id_type=MESH
        )

    def exchange(n, me, dev, src, dst, ssem, rsem):
        def copy(member, slot):
            return remote(src(member), dst(slot), ssem.at[member], rsem.at[slot], dev(member))

        def loop(body):
            def run(k, _):
                body(lax.rem(me + k, n))
                return 0

            lax.fori_loop(1, n, run, 0)

        return (
            lambda: loop(lambda m: copy(m, me).start()),
            lambda: loop(lambda m: copy(m, m).wait_recv()),
            lambda: loop(lambda m: copy(m, me).wait_send()),
        )

    over_t = functools.partial(exchange, n_t, t, lambda m: (d, m))
    over_dp = functools.partial(exchange, n_dp, d, lambda m: (m, t))

    def block_rows(block):
        return pl.ds(pl.multiple_of(block * own_toks, own_toks), own_toks)

    def top_rows(block):
        return pl.ds(pl.multiple_of(block * own_toks, half), half)

    def low_rows(block):
        return pl.ds(pl.multiple_of(block * own_toks + half, half), half)

    def columns(j):
        return pl.ds(pl.multiple_of(j * width, width), width)

    def own_local(j):
        return pltpu.make_async_copy(g_hbm.at[:, columns(j)], g_all.at[j, block_rows(t), :], loc_sem.at[j])

    def own_to(j, which, dev):
        return remote(
            g_hbm.at[:, columns(j)], g_all.at[j, block_rows(t), :], ag_send.at[j, which], ag_recv.at[j, which], (d, dev)
        )

    def pass_on(j, which, rows, dev):
        ref = g_all.at[j, rows, :]
        return remote(ref, ref, ag_send.at[j, which], ag_recv.at[j, which], (d, dev))

    def start_own(j):
        own_to(j, 0, up).start()
        own_to(j, 1, down).start()
        own_to(j, 2, partner).start()
        own_local(j).start()

    def forward_near(j):
        pass_on(j, 0, block_rows(down), up).wait_recv()
        pass_on(j, 3, top_rows(down), up).start()
        pass_on(j, 5, block_rows(down), partner).start()
        pass_on(j, 1, block_rows(up), down).wait_recv()
        pass_on(j, 4, low_rows(up), down).start()
        pass_on(j, 6, block_rows(up), partner).start()

    def forward_far(j):
        pass_on(j, 3, top_rows(across), up).wait_recv()
        pass_on(j, 4, low_rows(across), down).wait_recv()
        pass_on(j, 7, block_rows(across), partner).start()

    def arrived(j):
        own_local(j).wait()
        pass_on(j, 2, block_rows(partner), partner).wait_recv()
        pass_on(j, 5, block_rows(other(down)), partner).wait_recv()
        pass_on(j, 6, block_rows(other(up)), partner).wait_recv()
        pass_on(j, 7, block_rows(other(across)), partner).wait_recv()

    def merged_out(j):
        return pltpu.make_async_copy(merged_ref.at[:, columns(j)], merged_hbm.at[:, columns(j)], out_sem.at[j])

    def product(j):
        def run(i, _):
            rows = pl.ds(pl.multiple_of(i * step, step), step)
            grad = mm(at_ref[rows, :], g_all[j])
            merged_ref[rows, columns(j)] = (grad + e_ref[rows, columns(j)].astype(F32)).astype(BF16)
            return 0

        lax.fori_loop(0, n_step, run, 0)
        merged_out(j).start()

    ahead = 3

    def chunk(j, _):
        @pl.when(j + ahead < n_chunk)
        def _():
            start_own(j + ahead)

        @pl.when(j + 1 < n_chunk)
        def _():
            forward_near(j + 1)

        forward_far(j)
        arrived(j)
        product(j)
        return 0

    done = 0

    def fill(count):
        nonlocal done
        count = min(count, n_chunk - done)
        if done == 0:
            forward_near(0)
        if count > 0:
            lax.fori_loop(done, done + count, chunk, 0)
        done += count

    load_b.wait()
    bb_ref[...] = jnp.concatenate([basis_ref[...], basis_ref[...]], axis=1)
    load_g.wait()
    gb_all[block_rows(t), :] = pair(mm(g_own[...], bb_ref[...]))
    pl.semaphore_wait(barrier, n_t - 1 + n_dp - 1)
    x1 = over_t(lambda m: gb_all.at[block_rows(t), :], lambda m: gb_all.at[block_rows(m), :], x1s, x1r)
    x1[0]()
    for j in range(min(ahead, n_chunk)):
        start_own(j)

    def error_term(i, _):
        load_e(i).wait()
        rows = pl.ds(pl.multiple_of(i * step, step), step)
        ep_ref[rows, :] = mm(e_ref[rows, :], bb_ref[...])
        return 0

    lax.fori_loop(0, n_step, error_term, 0)
    load_a.wait()
    lanes = 128
    whole = ffl // lanes

    def turn(i, _):
        at = pl.ds(pl.multiple_of(i * lanes, lanes), lanes)
        at_ref[at, :] = a_ref[:, at].T
        return 0

    lax.fori_loop(0, whole, turn, 0)
    if ffl % lanes:
        at_ref[whole * lanes :, :] = a_ref[:, whole * lanes :].T

    x1[1]()

    def left_term(i, _):
        rows = pl.ds(pl.multiple_of(i * step, step), step)
        p_send[rows, :] = pair(fold(mm(at_ref[rows, :], gb_all[...])) + ep_ref[rows, :])
        return 0

    lax.fori_loop(0, n_step, left_term, 0)
    if n_dp * part > ffl:
        p_send[ffl:, :] = jnp.zeros((n_dp * part - ffl, 2 * rank), BF16)

    def part_rows(m):
        return pl.ds(pl.multiple_of(m * part, 16), part)

    x2 = over_dp(lambda m: p_send.at[part_rows(m), :], lambda m: p_parts.at[m], x2s, x2r)
    x2[0]()
    p_parts[d] = p_send[part_rows(d), :]
    fill(FILL["left_sum"])
    x2[1]()
    total = p_parts[0].astype(F32)
    for m in range(1, n_dp):
        total = total + p_parts[m].astype(F32)
    p_all[part_rows(d), :] = pair(fold(total))
    x3 = over_dp(lambda m: p_all.at[part_rows(d), :], lambda m: p_all.at[part_rows(m), :], x3s, x3r)
    x3[0]()
    fill(FILL["left_rows"])
    x3[1]()

    gram = mm_tn(p_all[...], p_all[...])
    gram_all[t] = fold(gram[:rank] + gram[rank:])
    x4 = over_t(lambda m: gram_all.at[t], lambda m: gram_all.at[m], x4s, x4r)
    x4[0]()
    fill(FILL["gram"])
    x4[1]()
    gram = gram_all[0]
    for m in range(1, n_t):
        gram = gram + gram_all[m]

    row_id = lax.broadcasted_iota(jnp.int32, (rank, 2 * rank), 0)
    lane_id = lax.broadcasted_iota(jnp.int32, (rank, 2 * rank), 1)
    elim_ref[...] = jnp.where(lane_id < rank, gram, jnp.where(lane_id - rank == row_id, 1.0, 0.0))

    def eliminate(k, _):
        x = elim_ref[...]
        row = elim_ref[pl.ds(k, 1), :]
        col = jnp.sum(jnp.where(lane_id == k, x, 0.0), axis=1, keepdims=True)
        pivot = jnp.sum(jnp.where(lane_id[:1] == k, row, 0.0), axis=1, keepdims=True)
        factor = jnp.where(row_id > k, col / pivot, 0.0)
        elim_ref[...] = x - factor * row
        return 0

    lax.fori_loop(0, rank, eliminate, 0)
    x = elim_ref[...]
    diag = jnp.sum(jnp.where(lane_id == row_id, x, 0.0), axis=1, keepdims=True)
    x = x * lax.rsqrt(diag)
    inverse = jnp.where(lane_id < rank, pltpu.roll(x, rank, 1), x)
    high = inverse.astype(BF16)
    both = jnp.concatenate([high, (inverse - high.astype(F32)).astype(BF16)], axis=0)

    def hat(i, _):
        rows = pl.ds(pl.multiple_of(i * step, step), step)
        phat_out[rows, :] = fold(mm_nt(p_all[rows, :], both)).astype(BF16)
        return 0

    lax.fori_loop(0, n_step, hat, 0)

    def acts_term(m, _):
        rows = block_rows(m)
        y_send[rows, :] = pair(mm(a_ref[rows, :], phat_out[...]))
        return 0

    lax.fori_loop(0, n_t, acts_term, 0)
    x5 = over_t(lambda m: y_send.at[block_rows(m), :], lambda m: y_parts.at[m], x5s, x5r)
    x5[0]()
    y_parts[t] = y_send[block_rows(t), :]
    pt_ref[...] = phat_out[...].T

    def right_error(j, _):
        q_loc[:, columns(j)] = mm(pt_ref[:rank, :], e_ref[:, columns(j)])
        return 0

    lax.fori_loop(0, n_chunk, right_error, 0)
    x5[1]()
    y = y_parts[0].astype(F32)
    for m in range(1, n_t):
        y = y + y_parts[m].astype(F32)
    y = pair(fold(y))

    def right_term(j, _):
        term = mm_tn(y, g_own[:, columns(j)])
        q_send[:, columns(j)] = (q_loc[:, columns(j)] + term[:rank] + term[rank:]).astype(BF16)
        return 0

    lax.fori_loop(0, n_chunk, right_term, 0)

    def q_block(m):
        return (
            pl.ds(pl.multiple_of(lax.div(m, q_split) * q_rows, 16), q_rows),
            pl.ds(pl.multiple_of(lax.rem(m, q_split) * q_cols, 128), q_cols),
        )

    x6 = over_dp(lambda m: q_send.at[q_block(m)], lambda m: q_parts.at[m], x6s, x6r)
    x6[0]()
    q_parts[d] = q_send[q_block(d)]
    fill(FILL["right_sum"])
    x6[1]()
    q = q_parts[0].astype(F32)
    for m in range(1, n_dp):
        q = q + q_parts[m].astype(F32)
    q_cross[t] = q.astype(BF16)
    x7 = over_t(lambda m: q_cross.at[t], lambda m: q_cross.at[m], x7s, x7r)
    x7[0]()
    fill(FILL["right_cross"])
    x7[1]()
    q = q_cross[0].astype(F32)
    for m in range(1, n_t):
        q = q + q_cross[m].astype(F32)
    qt_out[q_block(d)] = (q / n_dp).astype(BF16)
    x8 = over_dp(lambda m: qt_out.at[q_block(d)], lambda m: qt_out.at[q_block(m)], x8s, x8r)
    x8[0]()
    fill(n_chunk)
    x8[1]()

    for each in (x1, x2, x3, x4, x5, x6, x7, x8):
        each[2]()

    def drain(j, _):
        own_to(j, 0, up).wait_send()
        own_to(j, 1, down).wait_send()
        own_to(j, 2, partner).wait_send()
        pass_on(j, 3, top_rows(down), up).wait_send()
        pass_on(j, 4, low_rows(up), down).wait_send()
        pass_on(j, 5, block_rows(down), partner).wait_send()
        pass_on(j, 6, block_rows(up), partner).wait_send()
        pass_on(j, 7, block_rows(across), partner).wait_send()
        merged_out(j).wait()
        return 0

    lax.fori_loop(0, n_chunk, drain, 0)


def final_kernel(cols, place_ref, merged_ref, phat_ref, qt_ref, update_ref, new_ref, slice_ref):
    rank = qt_ref.shape[0]

    @pl.when(pl.program_id(0) == 0)
    def _():
        moved = pltpu.roll(qt_ref[...].astype(F32), place_ref[0], 1)
        slice_ref[...] = moved[:, :cols].astype(BF16)

    phat = phat_ref[:, :rank]
    full = mm(phat, qt_ref[...])
    new_ref[0] = (merged_ref[...].astype(F32) - full).astype(BF16)
    update_ref[...] = mm(phat, slice_ref[...]).astype(BF16)


def shards(n_dp, n_t, acts, grads, error, basis):
    toks, ffl = acts.shape
    own_toks, d_model = grads.shape
    rank = basis.shape[1]
    width = CHUNK
    n_chunk = d_model // width
    part = -(-ffl // (16 * n_dp)) * 16
    q_split = split_of(n_dp)
    q_rows, q_cols = rank // q_split[0], d_model // q_split[1]
    dma = pltpu.SemaphoreType.DMA
    anywhere = pl.BlockSpec(memory_space=pl.ANY)
    vmem = pl.BlockSpec(memory_space=pltpu.VMEM)
    merged, phat, qt = pl.pallas_call(
        functools.partial(step_kernel, n_dp, n_t),
        out_shape=(
            jax.ShapeDtypeStruct((ffl, d_model), BF16),
            jax.ShapeDtypeStruct((ffl, 2 * rank), BF16),
            jax.ShapeDtypeStruct((rank, d_model), BF16),
        ),
        in_specs=[anywhere] * 4,
        out_specs=(anywhere, vmem, vmem),
        scratch_shapes=[
            pltpu.VMEM((toks, ffl), BF16),
            pltpu.VMEM((ffl, toks), BF16),
            pltpu.VMEM((ffl, d_model), BF16),
            pltpu.VMEM((own_toks, d_model), BF16),
            pltpu.VMEM((n_chunk, toks, width), BF16),
            pltpu.VMEM((d_model, rank), BF16),
            pltpu.VMEM((d_model, 2 * rank), BF16),
            pltpu.VMEM((ffl, d_model), BF16),
            pltpu.VMEM((toks, 2 * rank), BF16),
            pltpu.VMEM((ffl, 2 * rank), F32),
            pltpu.VMEM((n_dp * part, 2 * rank), BF16),
            pltpu.VMEM((n_dp, part, 2 * rank), BF16),
            pltpu.VMEM((n_dp * part, 2 * rank), BF16),
            pltpu.VMEM((n_t, rank, 2 * rank), F32),
            pltpu.VMEM((rank, 2 * rank), F32),
            pltpu.VMEM((2 * rank, ffl), BF16),
            pltpu.VMEM((toks, 2 * rank), BF16),
            pltpu.VMEM((n_t, own_toks, 2 * rank), BF16),
            pltpu.VMEM((rank, d_model), F32),
            pltpu.VMEM((rank, d_model), BF16),
            pltpu.VMEM((n_dp, q_rows, q_cols), BF16),
            pltpu.VMEM((n_t, q_rows, q_cols), BF16),
            dma((3 + ffl // rows_step(ffl),)),
            dma((n_chunk,)),
            dma((n_chunk,)),
            dma((n_chunk, 8)),
            dma((n_chunk, 8)),
        ]
        + [dma((n,)) for n in (n_t, n_dp, n_dp, n_t, n_t, n_dp, n_t, n_dp) for _ in range(2)],
        compiler_params=pltpu.CompilerParams(
            collective_id=0, has_side_effects=True, vmem_limit_bytes=56 * 2**20
        ),
    )(acts, grads, error, basis)

    cols = d_model // n_dp
    step = rows_step(ffl) // 2 if rows_step(ffl) % 32 == 0 else rows_step(ffl)
    place = lax.rem(d_model - lax.axis_index("dp") * cols, d_model).astype(jnp.int32).reshape(1)
    return pl.pallas_call(
        functools.partial(final_kernel, cols),
        grid=(ffl // step,),
        out_shape=(
            jax.ShapeDtypeStruct((ffl, cols), BF16),
            jax.ShapeDtypeStruct((1, ffl, d_model), BF16),
        ),
        in_specs=[
            pl.BlockSpec(memory_space=pltpu.SMEM),
            pl.BlockSpec((step, d_model), lambda i: (i, 0)),
            pl.BlockSpec((step, 2 * rank), lambda i: (i, 0)),
            pl.BlockSpec((rank, d_model), lambda i: (0, 0)),
        ],
        out_specs=(
            pl.BlockSpec((step, cols), lambda i: (i, 0)),
            pl.BlockSpec((1, step, d_model), lambda i: (0, i, 0)),
        ),
        scratch_shapes=[pltpu.VMEM((rank, cols), BF16)],
        compiler_params=pltpu.CompilerParams(vmem_limit_bytes=32 * 2**20),
    )(place, merged, phat, qt)


def solution(mesh):
    n_dp, n_t = mesh.shape["dp"], mesh.shape["tensor"]
    return jax.shard_map(
        functools.partial(shards, n_dp, n_t),
        mesh=mesh,
        in_specs=(P("dp", "tensor"), P(("dp", "tensor"), None), P("dp", "tensor", None), P()),
        out_specs=(P("tensor", "dp"), P("dp", "tensor", None)),
        check_vma=False,
    )
```

```python
import functools

import jax
import jax.numpy as jnp
from jax import lax
from jax.experimental import pallas as pl
from jax.experimental.pallas import tpu as pltpu
from jax.sharding import PartitionSpec as P

MESH = pl.DeviceIdType.MESH
F32 = jnp.float32
BF16 = jnp.bfloat16
CHUNK = 256
WIDE = 512
FILL = {"left_sum": 2, "left_rows": 3, "gram": 0, "right_sum": 2, "right_cross": 2}


def mm(a, b):
    return lax.dot_general(a, b, (((1,), (0,)), ((), ())), preferred_element_type=F32)


def mm_tn(a, b):
    return lax.dot_general(a, b, (((0,), (0,)), ((), ())), preferred_element_type=F32)


def mm_nt(a, b):
    return lax.dot_general(a, b, (((1,), (1,)), ((), ())), preferred_element_type=F32)


def fold(x):
    return x + pltpu.roll(x, x.shape[1] // 2, 1)


def fold_rows(x):
    half = x.shape[0] // 2
    return x[:half] + x[half:]


def pair(x):
    lane = lax.broadcasted_iota(jnp.int32, x.shape, 1)
    high = x.astype(BF16).astype(F32)
    return jnp.where(lane < x.shape[1] // 2, x, x - high).astype(BF16)


def pair_rows(x):
    high = x.astype(BF16)
    return jnp.concatenate([high, (x - high.astype(F32)).astype(BF16)], axis=0)


def split_of(n_dp):
    rows = 1
    while rows * rows < n_dp:
        rows *= 2
    return rows, n_dp // rows


def pieces(total, count):
    while total % (16 * count):
        count -= 1
    return count


def lane_of_diagonal(x, lane_id, row_id):
    return jnp.sum(jnp.where(lane_id == row_id, x, 0.0), axis=1, keepdims=True)


def step_kernel(
    n_dp, n_t,
    at_hbm, g_hbm, e_hbm, bt_hbm,
    merged_ref, phat_out, phat_t_out, qt_out,
    at_ref, e_ref, g_own, g_all, basis_ref, bb_ref,
    gb_all, ep_ref, p_send, p_parts, p_all, pt_ref, gram_all, elim_ref,
    y_send, y_parts, q_loc, q_send, q_parts, q_cross,
    load_sem, e_sem, loc_sem, ag_send, ag_recv,
    x1s, x1r, x2s, x2r, x3s, x3r, x4s, x4r, x5s, x5r, x6s, x6r, x7s, x7r, x8s, x8r,
):
    ffl, toks = at_ref.shape
    own_toks, d_model = g_own.shape
    n_chunk = g_all.shape[0]
    width = g_all.shape[2]
    rank = qt_out.shape[0]
    half = own_toks // 2
    part = p_parts.shape[1]
    q_rows, q_cols = q_parts.shape[1:]
    q_split = d_model // q_cols
    d = lax.axis_index("dp")
    t = lax.axis_index("tensor")
    core = lax.rem(t, 2)
    partner = t + 1 - 2 * core
    up = lax.rem(t + 2, n_t)
    down = lax.rem(t + n_t - 2, n_t)
    across = lax.rem(t + 4, n_t)

    def other(block):
        return block + 1 - 2 * lax.rem(block, 2)

    n_step = e_sem.shape[0]
    step = ffl // n_step
    load_g = pltpu.make_async_copy(g_hbm, g_own, load_sem.at[0])
    load_b = pltpu.make_async_copy(bt_hbm, basis_ref, load_sem.at[1])
    load_a = pltpu.make_async_copy(at_hbm, at_ref, load_sem.at[2])
    load_g.start()
    load_b.start()

    def load_e(i):
        rows = pl.ds(pl.multiple_of(i * step, step), step)
        return pltpu.make_async_copy(e_hbm.at[0, rows, :], e_ref.at[rows, :], e_sem.at[i])

    for i in range(n_step):
        load_e(i).start()
    load_a.start()

    barrier = pltpu.get_barrier_semaphore()

    def greet_t(k, _):
        pl.semaphore_signal(barrier, inc=1, device_id=(d, lax.rem(t + k, n_t)), device_id_type=MESH)
        return 0

    def greet_d(k, _):
        pl.semaphore_signal(barrier, inc=1, device_id=(lax.rem(d + k, n_dp), t), device_id_type=MESH)
        return 0

    lax.fori_loop(1, n_t, greet_t, 0)
    lax.fori_loop(1, n_dp, greet_d, 0)

    def remote(src, dst, ssem, rsem, dev):
        return pltpu.make_async_remote_copy(
            src_ref=src, dst_ref=dst, send_sem=ssem, recv_sem=rsem, device_id=dev, device_id_type=MESH
        )

    def exchange(n, me, dev, src, dst, ssem, rsem):
        def copy(member, slot):
            return remote(src(member), dst(slot), ssem.at[member], rsem.at[slot], dev(member))

        def loop(body):
            def run(k, _):
                body(lax.rem(me + k, n))
                return 0

            lax.fori_loop(1, n, run, 0)

        return (
            lambda: loop(lambda m: copy(m, me).start()),
            lambda: loop(lambda m: copy(m, m).wait_recv()),
            lambda: loop(lambda m: copy(m, me).wait_send()),
        )

    over_t = functools.partial(exchange, n_t, t, lambda m: (d, m))
    over_dp = functools.partial(exchange, n_dp, d, lambda m: (m, t))

    def block_rows(block):
        return pl.ds(pl.multiple_of(block * own_toks, own_toks), own_toks)

    def top_rows(block):
        return pl.ds(pl.multiple_of(block * own_toks, half), half)

    def low_rows(block):
        return pl.ds(pl.multiple_of(block * own_toks + half, half), half)

    def columns(j):
        return pl.ds(pl.multiple_of(j * width, width), width)

    def own_local(j):
        return pltpu.make_async_copy(g_hbm.at[:, columns(j)], g_all.at[j, block_rows(t), :], loc_sem.at[j])

    def own_to(j, which, dev):
        return remote(
            g_hbm.at[:, columns(j)], g_all.at[j, block_rows(t), :], ag_send.at[j, which], ag_recv.at[j, which], (d, dev)
        )

    def pass_on(j, which, rows, dev):
        ref = g_all.at[j, rows, :]
        return remote(ref, ref, ag_send.at[j, which], ag_recv.at[j, which], (d, dev))

    def start_own(j):
        own_to(j, 0, up).start()
        own_to(j, 1, down).start()
        own_to(j, 2, partner).start()
        own_local(j).start()

    def forward_near(j):
        pass_on(j, 0, block_rows(down), up).wait_recv()
        pass_on(j, 3, top_rows(down), up).start()
        pass_on(j, 5, block_rows(down), partner).start()
        pass_on(j, 1, block_rows(up), down).wait_recv()
        pass_on(j, 4, low_rows(up), down).start()
        pass_on(j, 6, block_rows(up), partner).start()

    def forward_far(j):
        pass_on(j, 3, top_rows(across), up).wait_recv()
        pass_on(j, 4, low_rows(across), down).wait_recv()
        pass_on(j, 7, block_rows(across), partner).start()

    def arrived(j):
        own_local(j).wait()
        pass_on(j, 2, block_rows(partner), partner).wait_recv()
        pass_on(j, 5, block_rows(other(down)), partner).wait_recv()
        pass_on(j, 6, block_rows(other(up)), partner).wait_recv()
        pass_on(j, 7, block_rows(other(across)), partner).wait_recv()

    def product(j):
        grad = mm(at_ref[...], g_all[j])
        merged_ref[:, columns(j)] = (grad + e_ref[:, columns(j)].astype(F32)).astype(BF16)

    ahead = 4

    def chunk(j, _):
        @pl.when(j + ahead < n_chunk)
        def _():
            start_own(j + ahead)

        @pl.when(j + 2 < n_chunk)
        def _():
            forward_near(j + 2)

        @pl.when(j + 1 < n_chunk)
        def _():
            forward_far(j + 1)

        arrived(j)
        product(j)
        return 0

    done = 0

    def fill(count):
        nonlocal done
        count = min(count, n_chunk - done)
        if done == 0:
            forward_near(0)
            forward_near(1)
            forward_far(0)
        if count > 0:
            lax.fori_loop(done, done + count, chunk, 0)
        done += count

    load_b.wait()
    bb_ref[...] = jnp.concatenate([basis_ref[...], basis_ref[...]], axis=0).T
    load_g.wait()
    gb_all[block_rows(t), :] = pair(mm(g_own[...], bb_ref[...]))
    pl.semaphore_wait(barrier, n_t - 1 + n_dp - 1)
    x1 = over_t(lambda m: gb_all.at[block_rows(t), :], lambda m: gb_all.at[block_rows(m), :], x1s, x1r)
    x1[0]()
    for j in range(min(ahead, n_chunk)):
        start_own(j)

    def error_term(i, _):
        load_e(i).wait()
        rows = pl.ds(pl.multiple_of(i * step, step), step)
        ep_ref[rows, :] = mm(e_ref[rows, :], bb_ref[...])
        return 0

    lax.fori_loop(0, n_step, error_term, 0)
    load_a.wait()

    x1[1]()

    p_send[:ffl, :] = pair(fold(mm(at_ref[...], gb_all[...])) + ep_ref[...])
    if n_dp * part > ffl:
        p_send[ffl:, :] = jnp.zeros((n_dp * part - ffl, 2 * rank), BF16)

    def part_rows(m):
        return pl.ds(pl.multiple_of(m * part, 16), part)

    x2 = over_dp(lambda m: p_send.at[part_rows(m), :], lambda m: p_parts.at[m], x2s, x2r)
    x2[0]()
    p_parts[d] = p_send[part_rows(d), :]
    fill(FILL["left_sum"])
    x2[1]()
    total = p_parts[0].astype(F32)
    for m in range(1, n_dp):
        total = total + p_parts[m].astype(F32)
    p_all[part_rows(d), :] = pair(fold(total))
    x3 = over_dp(lambda m: p_all.at[part_rows(d), :], lambda m: p_all.at[part_rows(m), :], x3s, x3r)
    x3[0]()
    fill(FILL["left_rows"])
    x3[1]()

    pt_ref[...] = p_all[:ffl, :].T
    gram = fold(fold_rows(mm(pt_ref[...], p_all[:ffl, :])))
    lane_id = lax.broadcasted_iota(jnp.int32, (rank, 2 * rank), 1)
    row_id = lax.broadcasted_iota(jnp.int32, (rank, 2 * rank), 0)
    gram_all[t] = jnp.where(lane_id[: rank // 2] < rank, gram[: rank // 2], gram[rank // 2 :])
    x4 = over_t(lambda m: gram_all.at[t], lambda m: gram_all.at[m], x4s, x4r)
    x4[0]()
    y = pair_rows(fold_rows(mm(pt_ref[...], at_ref[...])))
    for m in range(n_t):
        y_send[m] = y[:, m * own_toks : (m + 1) * own_toks]
    x5 = over_t(lambda m: y_send.at[m], lambda m: y_parts.at[m], x5s, x5r)
    x5[0]()
    y_parts[t] = y_send[t]

    wide = min(WIDE, d_model)

    def wide_columns(j):
        return pl.ds(pl.multiple_of(j * wide, wide), wide)

    def right_error(j, _):
        q_loc[:, wide_columns(j)] = fold_rows(mm(pt_ref[...], e_ref[:, wide_columns(j)]))
        return 0

    lax.fori_loop(0, d_model // wide, right_error, 0)
    fill(FILL["gram"])
    x4[1]()

    gram = gram_all[0]
    for m in range(1, n_t):
        gram = gram + gram_all[m]
    gram = jnp.concatenate([gram, pltpu.roll(gram, rank, 1)], axis=0)
    elim_ref[...] = jnp.where(lane_id < rank, gram, jnp.where(lane_id - rank == row_id, 1.0, 0.0))
    group = 4

    def lane_of(x, k):
        return jnp.sum(jnp.where(lane_id[: x.shape[0]] == k, x, 0.0), axis=1, keepdims=True)

    def eliminate(i, _):
        k = i * group
        x = elim_ref[...]
        rows = [elim_ref[pl.ds(k + a, 1), :] for a in range(group)]
        cols = [lane_of(x, k + a) for a in range(group)]
        corner = [[lane_of(rows[a], k + b) for b in range(group)] for a in range(group)]
        for a in range(group):
            scale = 1.0 / corner[a][a]
            x = x - jnp.where(row_id > k + a, cols[a] * scale, 0.0) * rows[a]
            for b in range(a + 1, group):
                weight = corner[a][b] * scale
                cols[b] = cols[b] - cols[a] * weight
                rows[b] = rows[b] - rows[a] * weight
                for c in range(b, group):
                    corner[b][c] = corner[b][c] - corner[a][c] * weight
        elim_ref[...] = x
        return 0

    lax.fori_loop(0, rank // group, eliminate, 0)
    x = elim_ref[...]
    x = x * lax.rsqrt(lane_of_diagonal(x, lane_id, row_id))
    both = pair_rows(jnp.where(lane_id < rank, pltpu.roll(x, rank, 1), x))

    x5[1]()
    y = y_parts[0].astype(F32)
    for m in range(1, n_t):
        y = y + y_parts[m].astype(F32)
    y = pair_rows(fold_rows(y))

    def right_term(j, _):
        raw = q_loc[:, wide_columns(j)] + fold_rows(mm(y, g_own[:, wide_columns(j)]))
        q_send[:, wide_columns(j)] = fold_rows(mm(both, pair_rows(raw))).astype(BF16)
        return 0

    lax.fori_loop(0, d_model // wide, right_term, 0)

    def q_block(m):
        return (
            pl.ds(pl.multiple_of(lax.div(m, q_split) * q_rows, 16), q_rows),
            pl.ds(pl.multiple_of(lax.rem(m, q_split) * q_cols, 128), q_cols),
        )

    x6 = over_dp(lambda m: q_send.at[q_block(m)], lambda m: q_parts.at[m], x6s, x6r)
    x6[0]()
    q_parts[d] = q_send[q_block(d)]
    phat_out[...] = fold(mm_nt(p_all[:ffl, :], both)).astype(BF16)
    phat_t_out[...] = fold_rows(mm(both, pt_ref[...])).astype(BF16)
    fill(FILL["right_sum"])
    x6[1]()
    q = q_parts[0].astype(F32)
    for m in range(1, n_dp):
        q = q + q_parts[m].astype(F32)
    q_cross[t] = q.astype(BF16)
    x7 = over_t(lambda m: q_cross.at[t], lambda m: q_cross.at[m], x7s, x7r)
    x7[0]()
    fill(FILL["right_cross"])
    x7[1]()
    q = q_cross[0].astype(F32)
    for m in range(1, n_t):
        q = q + q_cross[m].astype(F32)
    qt_out[q_block(d)] = (q / n_dp).astype(BF16)
    x8 = over_dp(lambda m: qt_out.at[q_block(d)], lambda m: qt_out.at[q_block(m)], x8s, x8r)
    x8[0]()
    fill(n_chunk)
    x8[1]()

    for each in (x1, x2, x3, x4, x5, x6, x7, x8):
        each[2]()

    def drain(j, _):
        own_to(j, 0, up).wait_send()
        own_to(j, 1, down).wait_send()
        own_to(j, 2, partner).wait_send()
        pass_on(j, 3, top_rows(down), up).wait_send()
        pass_on(j, 4, low_rows(up), down).wait_send()
        pass_on(j, 5, block_rows(down), partner).wait_send()
        pass_on(j, 6, block_rows(up), partner).wait_send()
        pass_on(j, 7, block_rows(across), partner).wait_send()
        return 0

    lax.fori_loop(0, n_chunk, drain, 0)


def final_kernel(
    merged_ref, phat_ref, phat_t_ref, qt_ref, update_hbm, new_hbm, update_ref, new_ref, update_sem, new_sem
):
    rank, d_model = qt_ref.shape
    cols, ffl = update_ref.shape
    n_step = new_sem.shape[0]
    step = ffl // n_step

    def out(i):
        rows = pl.ds(pl.multiple_of(i * step, step), step)
        return pltpu.make_async_copy(new_ref.at[rows, :], new_hbm.at[0, rows, :], new_sem.at[i])

    def work(i, _):
        rows = pl.ds(pl.multiple_of(i * step, step), step)
        full = mm(phat_ref[rows, :rank], qt_ref[...])
        new_ref[rows, :] = (merged_ref[rows, :].astype(F32) - full).astype(BF16)
        out(i).start()
        return 0

    lax.fori_loop(0, n_step, work, 0)
    shift = lax.rem(d_model - lax.axis_index("dp") * cols, d_model)
    moved = pltpu.roll(qt_ref[...].astype(F32), shift, 1)
    update_ref[...] = mm_tn(moved[:, :cols].astype(BF16), phat_t_ref[...]).astype(BF16)
    update = pltpu.make_async_copy(update_ref, update_hbm, update_sem)
    update.start()

    def ended(i, _):
        out(i).wait()
        return 0

    lax.fori_loop(0, n_step, ended, 0)
    update.wait()


def shards(n_dp, n_t, acts, grads, error, basis):
    ffl, toks = acts.shape[1], acts.shape[0]
    own_toks, d_model = grads.shape
    rank = basis.shape[1]
    width = CHUNK
    n_chunk = d_model // width
    part = -(-ffl // (16 * n_dp)) * 16
    q_split = split_of(n_dp)
    q_rows, q_cols = rank // q_split[0], d_model // q_split[1]
    dma = pltpu.SemaphoreType.DMA
    anywhere = pl.BlockSpec(memory_space=pltpu.HBM)
    vmem = pl.BlockSpec(memory_space=pltpu.VMEM)
    factors = pl.pallas_call(
        functools.partial(step_kernel, n_dp, n_t),
        out_shape=(
            pltpu.VMEM((ffl, d_model), BF16),
            pltpu.VMEM((ffl, 2 * rank), BF16),
            pltpu.VMEM((rank, ffl), BF16),
            pltpu.VMEM((rank, d_model), BF16),
        ),
        in_specs=[anywhere] * 4,
        out_specs=(vmem,) * 4,
        scratch_shapes=[
            pltpu.VMEM((ffl, toks), BF16),
            pltpu.VMEM((ffl, d_model), BF16),
            pltpu.VMEM((own_toks, d_model), BF16),
            pltpu.VMEM((n_chunk, toks, width), BF16),
            pltpu.VMEM((rank, d_model), BF16),
            pltpu.VMEM((d_model, 2 * rank), BF16),
            pltpu.VMEM((toks, 2 * rank), BF16),
            pltpu.VMEM((ffl, 2 * rank), F32),
            pltpu.VMEM((n_dp * part, 2 * rank), BF16),
            pltpu.VMEM((n_dp, part, 2 * rank), BF16),
            pltpu.VMEM((n_dp * part, 2 * rank), BF16),
            pltpu.VMEM((2 * rank, ffl), BF16),
            pltpu.VMEM((n_t, rank // 2, 2 * rank), F32),
            pltpu.VMEM((rank, 2 * rank), F32),
            pltpu.VMEM((n_t, 2 * rank, own_toks), BF16),
            pltpu.VMEM((n_t, 2 * rank, own_toks), BF16),
            pltpu.VMEM((rank, d_model), F32),
            pltpu.VMEM((rank, d_model), BF16),
            pltpu.VMEM((n_dp, q_rows, q_cols), BF16),
            pltpu.VMEM((n_t, q_rows, q_cols), BF16),
            dma((3,)),
            dma((pieces(ffl, 2),)),
            dma((n_chunk,)),
            dma((n_chunk, 8)),
            dma((n_chunk, 8)),
        ]
        + [dma((n,)) for n in (n_t, n_dp, n_dp, n_t, n_t, n_dp, n_t, n_dp) for _ in range(2)],
        compiler_params=pltpu.CompilerParams(
            collective_id=0, has_side_effects=True, vmem_limit_bytes=55 * 2**20
        ),
    )(acts.T, grads, error, basis.T)

    cols = d_model // n_dp
    update, new_error = pl.pallas_call(
        final_kernel,
        out_shape=(
            jax.ShapeDtypeStruct((cols, ffl), BF16),
            jax.ShapeDtypeStruct((1, ffl, d_model), BF16),
        ),
        in_specs=[vmem] * 4,
        out_specs=(anywhere,) * 2,
        scratch_shapes=[
            pltpu.VMEM((cols, ffl), BF16),
            pltpu.VMEM((ffl, d_model), BF16),
            dma,
            dma((pieces(ffl, 5),)),
        ],
        compiler_params=pltpu.CompilerParams(vmem_limit_bytes=40 * 2**20),
    )(*factors)
    return update.T, new_error


def solution(mesh):
    n_dp, n_t = mesh.shape["dp"], mesh.shape["tensor"]
    return jax.shard_map(
        functools.partial(shards, n_dp, n_t),
        mesh=mesh,
        in_specs=(P("dp", "tensor"), P(("dp", "tensor"), None), P("dp", "tensor", None), P()),
        out_specs=(P("tensor", "dp"), P("dp", "tensor", None)),
        check_vma=False,
    )
```

```python
import functools

import jax
import jax.numpy as jnp
from jax import lax
from jax.experimental import pallas as pl
from jax.experimental.pallas import tpu as pltpu
from jax.sharding import PartitionSpec as P

MESH = pl.DeviceIdType.MESH
F32 = jnp.float32
BF16 = jnp.bfloat16
CHUNK = 256
WIDE = 512
AHEAD = 4
SERVE = {"error": 1, "left_sum": 1, "left_rows": 0, "gram": 1, "inverse": 1}
FILL = {"left_sum": 0, "left_rows": 2, "gram": 0, "right_sum": 3, "right_cross": 2}


def mm(a, b):
    return lax.dot_general(a, b, (((1,), (0,)), ((), ())), preferred_element_type=F32)


def mm_tn(a, b):
    return lax.dot_general(a, b, (((0,), (0,)), ((), ())), preferred_element_type=F32)


def mm_nt(a, b):
    return lax.dot_general(a, b, (((1,), (1,)), ((), ())), preferred_element_type=F32)


def fold(x):
    return x + pltpu.roll(x, x.shape[1] // 2, 1)


def fold_rows(x):
    half = x.shape[0] // 2
    return x[:half] + x[half:]


def pair(x):
    lane = lax.broadcasted_iota(jnp.int32, x.shape, 1)
    high = x.astype(BF16).astype(F32)
    return jnp.where(lane < x.shape[1] // 2, x, x - high).astype(BF16)


def pair_rows(x):
    high = x.astype(BF16)
    return jnp.concatenate([high, (x - high.astype(F32)).astype(BF16)], axis=0)


def split_of(n_dp):
    rows = 1
    while rows * rows < n_dp:
        rows *= 2
    return rows, n_dp // rows


def pieces(total, count):
    while total % (16 * count):
        count -= 1
    return count


def lane_of_diagonal(x, lane_id, row_id):
    return jnp.sum(jnp.where(lane_id == row_id, x, 0.0), axis=1, keepdims=True)


def step_kernel(
    n_dp, n_t,
    at_hbm, g_hbm, e_hbm, bt_hbm,
    merged_ref, phat_out, phat_t_out, qt_out,
    at_ref, e_ref, g_own, g_all, basis_ref, bb_ref,
    gb_all, ep_ref, p_send, p_parts, p_all, pt_ref, gram_all, elim_ref,
    y_send, y_parts, q_loc, q_send, q_parts, q_cross,
    load_sem, e_sem, loc_sem, ag_send, ag_recv,
    x1s, x1r, x2s, x2r, x3s, x3r, x4s, x4r, x5s, x5r, x6s, x6r, x7s, x7r, x8s, x8r,
):
    ffl, toks = at_ref.shape
    own_toks, d_model = g_own.shape
    n_chunk = g_all.shape[0]
    width = g_all.shape[2]
    rank = qt_out.shape[0]
    half = own_toks // 2
    part = p_parts.shape[1]
    q_rows, q_cols = q_parts.shape[1:]
    q_split = d_model // q_cols
    d = lax.axis_index("dp")
    t = lax.axis_index("tensor")
    core = lax.rem(t, 2)
    partner = t + 1 - 2 * core
    up = lax.rem(t + 2, n_t)
    down = lax.rem(t + n_t - 2, n_t)
    across = lax.rem(t + 4, n_t)

    def other(block):
        return block + 1 - 2 * lax.rem(block, 2)

    barrier = pltpu.get_barrier_semaphore()

    def greet_t(k, _):
        pl.semaphore_signal(barrier, inc=1, device_id=(d, lax.rem(t + k, n_t)), device_id_type=MESH)
        return 0

    def greet_d(k, _):
        pl.semaphore_signal(barrier, inc=1, device_id=(lax.rem(d + k, n_dp), t), device_id_type=MESH)
        return 0

    lax.fori_loop(1, n_t, greet_t, 0)
    lax.fori_loop(1, n_dp, greet_d, 0)

    n_step = e_sem.shape[0]
    step = ffl // n_step
    load_g = pltpu.make_async_copy(g_hbm, g_own, load_sem.at[0])
    load_b = pltpu.make_async_copy(bt_hbm, basis_ref, load_sem.at[1])
    load_a = pltpu.make_async_copy(at_hbm, at_ref, load_sem.at[2])
    load_g.start()
    load_b.start()

    def load_e(i):
        rows = pl.ds(pl.multiple_of(i * step, step), step)
        return pltpu.make_async_copy(e_hbm.at[0, rows, :], e_ref.at[rows, :], e_sem.at[i])

    for i in range(n_step):
        load_e(i).start()
    load_a.start()

    def remote(src, dst, ssem, rsem, dev):
        return pltpu.make_async_remote_copy(
            src_ref=src, dst_ref=dst, send_sem=ssem, recv_sem=rsem, device_id=dev, device_id_type=MESH
        )

    def exchange(n, me, dev, src, dst, ssem, rsem):
        def copy(member, slot):
            return remote(src(member), dst(slot), ssem.at[member], rsem.at[slot], dev(member))

        def loop(body):
            def run(k, _):
                body(lax.rem(me + k, n))
                return 0

            lax.fori_loop(1, n, run, 0)

        return (
            lambda: loop(lambda m: copy(m, me).start()),
            lambda: loop(lambda m: copy(m, m).wait_recv()),
            lambda: loop(lambda m: copy(m, me).wait_send()),
        )

    over_t = functools.partial(exchange, n_t, t, lambda m: (d, m))
    over_dp = functools.partial(exchange, n_dp, d, lambda m: (m, t))

    def block_rows(block):
        return pl.ds(pl.multiple_of(block * own_toks, own_toks), own_toks)

    def top_rows(block):
        return pl.ds(pl.multiple_of(block * own_toks, half), half)

    def low_rows(block):
        return pl.ds(pl.multiple_of(block * own_toks + half, half), half)

    def columns(j):
        return pl.ds(pl.multiple_of(j * width, width), width)

    def own_local(j):
        return pltpu.make_async_copy(g_hbm.at[:, columns(j)], g_all.at[j, block_rows(t), :], loc_sem.at[j])

    def own_to(j, which, dev):
        return remote(
            g_hbm.at[:, columns(j)], g_all.at[j, block_rows(t), :], ag_send.at[j, which], ag_recv.at[j, which], (d, dev)
        )

    def pass_on(j, which, rows, dev):
        ref = g_all.at[j, rows, :]
        return remote(ref, ref, ag_send.at[j, which], ag_recv.at[j, which], (d, dev))

    def start_own(j):
        own_to(j, 0, up).start()
        own_to(j, 1, down).start()
        own_to(j, 2, partner).start()
        own_local(j).start()

    def forward_near(j):
        pass_on(j, 0, block_rows(down), up).wait_recv()
        pass_on(j, 3, top_rows(down), up).start()
        pass_on(j, 5, block_rows(down), partner).start()
        pass_on(j, 1, block_rows(up), down).wait_recv()
        pass_on(j, 4, low_rows(up), down).start()
        pass_on(j, 6, block_rows(up), partner).start()

    def forward_far(j):
        pass_on(j, 3, top_rows(across), up).wait_recv()
        pass_on(j, 4, low_rows(across), down).wait_recv()
        pass_on(j, 7, block_rows(across), partner).start()

    def arrived(j):
        own_local(j).wait()
        pass_on(j, 2, block_rows(partner), partner).wait_recv()
        pass_on(j, 5, block_rows(other(down)), partner).wait_recv()
        pass_on(j, 6, block_rows(other(up)), partner).wait_recv()
        pass_on(j, 7, block_rows(other(across)), partner).wait_recv()

    def product(j):
        grad = mm(at_ref[...], g_all[j])
        merged_ref[:, columns(j)] = (grad + e_ref[:, columns(j)].astype(F32)).astype(BF16)

    def serve_step(j):
        @pl.when(j + AHEAD < n_chunk)
        def _():
            start_own(j + AHEAD)

        @pl.when(j < n_chunk)
        def _():
            forward_near(j)

        @pl.when(j > 0 and j <= n_chunk if isinstance(j, int) else (j > 0) & (j <= n_chunk))
        def _():
            forward_far(j - 1)

    served = 0
    done = 0

    def serve(count):
        nonlocal served
        count = min(count, n_chunk + 1 - served)
        for j in range(served, served + count):
            serve_step(j)
        served += count

    def fill(count):
        nonlocal served, done
        count = min(count, n_chunk - done)
        lead = served - done

        def chunk(j, _):
            serve_step(j + lead)
            arrived(j)
            product(j)
            return 0

        if count > 0:
            lax.fori_loop(done, done + count, chunk, 0)
        done += count
        served = min(served + count, n_chunk + 1)

    load_b.wait()
    twice = jnp.concatenate([basis_ref[...], basis_ref[...]], axis=0)
    load_g.wait()
    gb_all[block_rows(t), :] = pair(mm_nt(g_own[...], twice))
    pl.semaphore_wait(barrier, n_t - 1 + n_dp - 1)
    x1 = over_t(lambda m: gb_all.at[block_rows(t), :], lambda m: gb_all.at[block_rows(m), :], x1s, x1r)
    x1[0]()
    for j in range(min(AHEAD, n_chunk)):
        start_own(j)

    bb_ref[...] = twice.T

    def error_term(i, _):
        load_e(i).wait()
        rows = pl.ds(pl.multiple_of(i * step, step), step)
        ep_ref[rows, :] = mm(e_ref[rows, :], bb_ref[...])
        return 0

    lax.fori_loop(0, n_step, error_term, 0)
    load_a.wait()
    serve(SERVE["error"])

    x1[1]()

    p_send[:ffl, :] = pair(fold(mm(at_ref[...], gb_all[...])) + ep_ref[...])
    if n_dp * part > ffl:
        p_send[ffl:, :] = jnp.zeros((n_dp * part - ffl, 2 * rank), BF16)

    def part_rows(m):
        return pl.ds(pl.multiple_of(m * part, 16), part)

    x2 = over_dp(lambda m: p_send.at[part_rows(m), :], lambda m: p_parts.at[m], x2s, x2r)
    x2[0]()
    p_parts[d] = p_send[part_rows(d), :]
    serve(SERVE["left_sum"])
    fill(FILL["left_sum"])
    x2[1]()
    total = p_parts[0].astype(F32)
    for m in range(1, n_dp):
        total = total + p_parts[m].astype(F32)
    p_all[part_rows(d), :] = pair(fold(total))
    x3 = over_dp(lambda m: p_all.at[part_rows(d), :], lambda m: p_all.at[part_rows(m), :], x3s, x3r)
    x3[0]()
    serve(SERVE["left_rows"])
    fill(FILL["left_rows"])
    x3[1]()

    pt_ref[...] = p_all[:ffl, :].T
    gram = fold(fold_rows(mm(pt_ref[...], p_all[:ffl, :])))
    lane_id = lax.broadcasted_iota(jnp.int32, (rank, 2 * rank), 1)
    row_id = lax.broadcasted_iota(jnp.int32, (rank, 2 * rank), 0)
    gram_all[t] = jnp.where(lane_id[: rank // 2] < rank, gram[: rank // 2], gram[rank // 2 :])
    x4 = over_t(lambda m: gram_all.at[t], lambda m: gram_all.at[m], x4s, x4r)
    x4[0]()
    y = pair_rows(fold_rows(mm(pt_ref[...], at_ref[...])))
    for m in range(n_t):
        y_send[m] = y[:, m * own_toks : (m + 1) * own_toks]
    x5 = over_t(lambda m: y_send.at[m], lambda m: y_parts.at[m], x5s, x5r)
    x5[0]()
    y_parts[t] = y_send[t]

    wide = min(WIDE, d_model)

    def wide_columns(j):
        return pl.ds(pl.multiple_of(j * wide, wide), wide)

    def right_error(j, _):
        q_loc[:, wide_columns(j)] = fold_rows(mm(pt_ref[...], e_ref[:, wide_columns(j)]))
        return 0

    lax.fori_loop(0, d_model // wide, right_error, 0)
    serve(SERVE["gram"])
    fill(FILL["gram"])
    x4[1]()

    gram = gram_all[0]
    for m in range(1, n_t):
        gram = gram + gram_all[m]
    gram = jnp.concatenate([gram, pltpu.roll(gram, rank, 1)], axis=0)
    elim_ref[...] = jnp.where(lane_id < rank, gram, jnp.where(lane_id - rank == row_id, 1.0, 0.0))
    group = 4

    def lane_of(x, k):
        return jnp.sum(jnp.where(lane_id[: x.shape[0]] == k, x, 0.0), axis=1, keepdims=True)

    def eliminate(i, _):
        k = i * group
        x = elim_ref[...]
        rows = [elim_ref[pl.ds(k + a, 1), :] for a in range(group)]
        cols = [lane_of(x, k + a) for a in range(group)]
        corner = [[lane_of(rows[a], k + b) for b in range(group)] for a in range(group)]
        for a in range(group):
            scale = 1.0 / corner[a][a]
            x = x - jnp.where(row_id > k + a, cols[a] * scale, 0.0) * rows[a]
            for b in range(a + 1, group):
                weight = corner[a][b] * scale
                cols[b] = cols[b] - cols[a] * weight
                rows[b] = rows[b] - rows[a] * weight
                for c in range(b, group):
                    corner[b][c] = corner[b][c] - corner[a][c] * weight
        elim_ref[...] = x
        return 0

    lax.fori_loop(0, rank // group, eliminate, 0)
    x = elim_ref[...]
    x = x * lax.rsqrt(lane_of_diagonal(x, lane_id, row_id))
    both = pair_rows(jnp.where(lane_id < rank, pltpu.roll(x, rank, 1), x))

    serve(SERVE["inverse"])

    x5[1]()
    y = y_parts[0].astype(F32)
    for m in range(1, n_t):
        y = y + y_parts[m].astype(F32)
    y = pair_rows(fold_rows(y))

    def right_term(j, _):
        raw = q_loc[:, wide_columns(j)] + fold_rows(mm(y, g_own[:, wide_columns(j)]))
        q_send[:, wide_columns(j)] = fold_rows(mm(both, pair_rows(raw))).astype(BF16)
        return 0

    lax.fori_loop(0, d_model // wide, right_term, 0)

    def q_block(m):
        return (
            pl.ds(pl.multiple_of(lax.div(m, q_split) * q_rows, 16), q_rows),
            pl.ds(pl.multiple_of(lax.rem(m, q_split) * q_cols, 128), q_cols),
        )

    x6 = over_dp(lambda m: q_send.at[q_block(m)], lambda m: q_parts.at[m], x6s, x6r)
    x6[0]()
    q_parts[d] = q_send[q_block(d)]
    phat_out[...] = fold(mm_nt(p_all[:ffl, :], both)).astype(BF16)
    phat_t_out[...] = fold_rows(mm(both, pt_ref[...])).astype(BF16)
    fill(FILL["right_sum"])
    x6[1]()
    q = q_parts[0].astype(F32)
    for m in range(1, n_dp):
        q = q + q_parts[m].astype(F32)
    q_cross[t] = q.astype(BF16)
    x7 = over_t(lambda m: q_cross.at[t], lambda m: q_cross.at[m], x7s, x7r)
    x7[0]()
    fill(FILL["right_cross"])
    x7[1]()
    q = q_cross[0].astype(F32)
    for m in range(1, n_t):
        q = q + q_cross[m].astype(F32)
    qt_out[q_block(d)] = (q / n_dp).astype(BF16)
    x8 = over_dp(lambda m: qt_out.at[q_block(d)], lambda m: qt_out.at[q_block(m)], x8s, x8r)
    x8[0]()
    fill(n_chunk)

    for each in (x1, x2, x3, x4, x5, x6, x7):
        each[2]()

    def drain(j, _):
        own_to(j, 0, up).wait_send()
        own_to(j, 1, down).wait_send()
        own_to(j, 2, partner).wait_send()
        pass_on(j, 3, top_rows(down), up).wait_send()
        pass_on(j, 4, low_rows(up), down).wait_send()
        pass_on(j, 5, block_rows(down), partner).wait_send()
        pass_on(j, 6, block_rows(up), partner).wait_send()
        pass_on(j, 7, block_rows(across), partner).wait_send()
        return 0

    lax.fori_loop(0, n_chunk, drain, 0)
    x8[1]()
    x8[2]()


def final_kernel(
    merged_ref, phat_ref, phat_t_ref, qt_ref, update_hbm, new_hbm, update_ref, new_ref, update_sem, new_sem
):
    rank, d_model = qt_ref.shape
    cols, ffl = update_ref.shape
    n_step = new_sem.shape[0]
    step = ffl // n_step

    def out(i):
        rows = pl.ds(pl.multiple_of(i * step, step), step)
        return pltpu.make_async_copy(new_ref.at[rows, :], new_hbm.at[0, rows, :], new_sem.at[i])

    def work(i, _):
        rows = pl.ds(pl.multiple_of(i * step, step), step)
        full = mm(phat_ref[rows, :rank], qt_ref[...])
        new_ref[rows, :] = (merged_ref[rows, :].astype(F32) - full).astype(BF16)
        out(i).start()
        return 0

    lax.fori_loop(0, n_step, work, 0)
    shift = lax.rem(d_model - lax.axis_index("dp") * cols, d_model)
    moved = pltpu.roll(qt_ref[...].astype(F32), shift, 1)
    update_ref[...] = mm_tn(moved[:, :cols].astype(BF16), phat_t_ref[...]).astype(BF16)
    update = pltpu.make_async_copy(update_ref, update_hbm, update_sem)
    update.start()

    def ended(i, _):
        out(i).wait()
        return 0

    lax.fori_loop(0, n_step, ended, 0)
    update.wait()


def shards(n_dp, n_t, acts, grads, error, basis):
    ffl, toks = acts.shape[1], acts.shape[0]
    own_toks, d_model = grads.shape
    rank = basis.shape[1]
    width = CHUNK
    n_chunk = d_model // width
    part = -(-ffl // (16 * n_dp)) * 16
    q_split = split_of(n_dp)
    q_rows, q_cols = rank // q_split[0], d_model // q_split[1]
    dma = pltpu.SemaphoreType.DMA
    anywhere = pl.BlockSpec(memory_space=pltpu.HBM)
    vmem = pl.BlockSpec(memory_space=pltpu.VMEM)
    factors = pl.pallas_call(
        functools.partial(step_kernel, n_dp, n_t),
        out_shape=(
            pltpu.VMEM((ffl, d_model), BF16),
            pltpu.VMEM((ffl, 2 * rank), BF16),
            pltpu.VMEM((rank, ffl), BF16),
            pltpu.VMEM((rank, d_model), BF16),
        ),
        in_specs=[anywhere] * 4,
        out_specs=(vmem,) * 4,
        scratch_shapes=[
            pltpu.VMEM((ffl, toks), BF16),
            pltpu.VMEM((ffl, d_model), BF16),
            pltpu.VMEM((own_toks, d_model), BF16),
            pltpu.VMEM((n_chunk, toks, width), BF16),
            pltpu.VMEM((rank, d_model), BF16),
            pltpu.VMEM((d_model, 2 * rank), BF16),
            pltpu.VMEM((toks, 2 * rank), BF16),
            pltpu.VMEM((ffl, 2 * rank), F32),
            pltpu.VMEM((n_dp * part, 2 * rank), BF16),
            pltpu.VMEM((n_dp, part, 2 * rank), BF16),
            pltpu.VMEM((n_dp * part, 2 * rank), BF16),
            pltpu.VMEM((2 * rank, ffl), BF16),
            pltpu.VMEM((n_t, rank // 2, 2 * rank), F32),
            pltpu.VMEM((rank, 2 * rank), F32),
            pltpu.VMEM((n_t, 2 * rank, own_toks), BF16),
            pltpu.VMEM((n_t, 2 * rank, own_toks), BF16),
            pltpu.VMEM((rank, d_model), F32),
            pltpu.VMEM((rank, d_model), BF16),
            pltpu.VMEM((n_dp, q_rows, q_cols), BF16),
            pltpu.VMEM((n_t, q_rows, q_cols), BF16),
            dma((3,)),
            dma((pieces(ffl, 2),)),
            dma((n_chunk,)),
            dma((n_chunk, 8)),
            dma((n_chunk, 8)),
        ]
        + [dma((n,)) for n in (n_t, n_dp, n_dp, n_t, n_t, n_dp, n_t, n_dp) for _ in range(2)],
        compiler_params=pltpu.CompilerParams(
            collective_id=0, has_side_effects=True, vmem_limit_bytes=55 * 2**20
        ),
    )(acts.T, grads, error, basis.T)

    cols = d_model // n_dp
    update, new_error = pl.pallas_call(
        final_kernel,
        out_shape=(
            jax.ShapeDtypeStruct((cols, ffl), BF16),
            jax.ShapeDtypeStruct((1, ffl, d_model), BF16),
        ),
        in_specs=[vmem] * 4,
        out_specs=(anywhere,) * 2,
        scratch_shapes=[
            pltpu.VMEM((cols, ffl), BF16),
            pltpu.VMEM((ffl, d_model), BF16),
            dma,
            dma((pieces(ffl, 5),)),
        ],
        compiler_params=pltpu.CompilerParams(vmem_limit_bytes=40 * 2**20),
    )(*factors)
    return update.T, new_error


def solution(mesh):
    n_dp, n_t = mesh.shape["dp"], mesh.shape["tensor"]
    return jax.shard_map(
        functools.partial(shards, n_dp, n_t),
        mesh=mesh,
        in_specs=(P("dp", "tensor"), P(("dp", "tensor"), None), P("dp", "tensor", None), P()),
        out_specs=(P("tensor", "dp"), P("dp", "tensor", None)),
        check_vma=False,
    )
```

```python
import functools

import jax
import jax.numpy as jnp
from jax import lax
from jax.experimental import pallas as pl
from jax.experimental.pallas import tpu as pltpu
from jax.sharding import PartitionSpec as P

MESH = pl.DeviceIdType.MESH
F32 = jnp.float32
BF16 = jnp.bfloat16
CHUNK = 256
WIDE = 512
AHEAD = 4
SERVE = {"error": 1, "left_sum": 1, "left_rows": 0, "gram": 1, "inverse": 1}
FILL = {"left_sum": 0, "left_rows": 2, "gram": 0, "right_sum": 2, "right_cross": 2}


def mm(a, b):
    return lax.dot_general(a, b, (((1,), (0,)), ((), ())), preferred_element_type=F32)


def mm_tn(a, b):
    return lax.dot_general(a, b, (((0,), (0,)), ((), ())), preferred_element_type=F32)


def mm_nt(a, b):
    return lax.dot_general(a, b, (((1,), (1,)), ((), ())), preferred_element_type=F32)


def fold(x):
    return x + pltpu.roll(x, x.shape[1] // 2, 1)


def fold_rows(x):
    half = x.shape[0] // 2
    return x[:half] + x[half:]


def pair(x):
    lane = lax.broadcasted_iota(jnp.int32, x.shape, 1)
    high = x.astype(BF16).astype(F32)
    return jnp.where(lane < x.shape[1] // 2, x, x - high).astype(BF16)


def pair_rows(x):
    high = x.astype(BF16)
    return jnp.concatenate([high, (x - high.astype(F32)).astype(BF16)], axis=0)


def split_of(n_dp):
    rows = 1
    while rows * rows < n_dp:
        rows *= 2
    return rows, n_dp // rows


def pieces(total, count):
    while total % (16 * count):
        count -= 1
    return count


def lane_of_diagonal(x, lane_id, row_id):
    return jnp.sum(jnp.where(lane_id == row_id, x, 0.0), axis=1, keepdims=True)


def step_kernel(
    n_dp, n_t, n_y, n_x,
    at_hbm, g_hbm, e_hbm, bt_hbm,
    merged_ref, phat_out, phat_t_out, qt_out,
    at_ref, e_ref, g_own, g_all, basis_ref, bb_ref,
    gbt_all, gb_all, ep_ref, p_send, p_parts, p_all, pt_ref, gram_all, elim_ref,
    y_send, y_parts, q_loc, q_send, q_parts, q_cross,
    load_sem, e_sem, loc_sem, ag_send, ag_recv,
    x1s, x1r, x2s, x2r, x3s, x3r, x4s, x4r, x5s, x5r, x6s, x6r, x7s, x7r, x8s, x8r,
):
    toks = at_ref.shape[1]
    ffl = merged_ref.shape[0]
    own_toks, d_model = g_own.shape
    n_chunk = g_all.shape[0]
    width = g_all.shape[2]
    rank = qt_out.shape[0]
    half = own_toks // 2
    part = p_parts.shape[1]
    q_rows, q_cols = q_parts.shape[1:]
    d = lax.axis_index("dp")
    t = lax.axis_index("tensor")
    y, x = lax.div(d, n_x), lax.rem(d, n_x)
    core = lax.rem(t, 2)
    partner = t + 1 - 2 * core
    up = lax.rem(t + 2, n_t)
    down = lax.rem(t + n_t - 2, n_t)
    across = lax.rem(t + 4, n_t)

    def other(block):
        return block + 1 - 2 * lax.rem(block, 2)


    barrier = pltpu.get_barrier_semaphore()

    def greet_t(k, _):
        pl.semaphore_signal(barrier, inc=1, device_id=(d, lax.rem(t + k, n_t)), device_id_type=MESH)
        return 0

    def greet_d(k, _):
        pl.semaphore_signal(barrier, inc=1, device_id=(lax.rem(d + k, n_dp), t), device_id_type=MESH)
        return 0

    lax.fori_loop(1, n_t, greet_t, 0)
    lax.fori_loop(1, n_dp, greet_d, 0)

    n_step = e_sem.shape[0]
    step = ffl // n_step
    load_g = pltpu.make_async_copy(g_hbm, g_own, load_sem.at[0])
    load_b = pltpu.make_async_copy(bt_hbm, basis_ref, load_sem.at[1])
    load_a = pltpu.make_async_copy(at_hbm, at_ref.at[:ffl, :], load_sem.at[2])
    load_g.start()
    load_b.start()

    def load_e(i):
        rows = pl.ds(pl.multiple_of(i * step, step), step)
        return pltpu.make_async_copy(e_hbm.at[0, rows, :], e_ref.at[rows, :], e_sem.at[i])

    for i in range(n_step):
        load_e(i).start()
    load_a.start()

    def remote(src, dst, ssem, rsem, dev):
        return pltpu.make_async_remote_copy(
            src_ref=src, dst_ref=dst, send_sem=ssem, recv_sem=rsem, device_id=dev, device_id_type=MESH
        )

    def place(dy, dx):
        return lax.rem(y + dy, n_y) * n_x + lax.rem(x + dx, n_x)

    def hops(dy, dx):
        return min(dy, n_y - dy) + min(dx, n_x - dx)

    offsets = [(dy, dx) for dy in range(n_y) for dx in range(n_x) if dy or dx]
    dp_order = [place(*o) for o in sorted(offsets, key=lambda o: hops(*o))]
    dp_near = sum(hops(*o) < 3 for o in offsets)
    t_order = [partner, up, down, other(up), other(down), across, other(across)]
    t_near = 5

    class Exchange:
        def __init__(self, me, order, near, dev, src, dst, ssem, rsem):
            self.me, self.order, self.near = me, order, near
            self.copy = lambda member, slot: remote(src(member), dst(slot), ssem.at[member], rsem.at[slot], dev(member))

        def start_one(self, member):
            self.copy(member, self.me).start()

        def start(self):
            for member in self.order:
                self.start_one(member)

        def received(self, members=None):
            for member in self.order if members is None else members:
                self.copy(member, member).wait_recv()

        def sent(self):
            for member in self.order:
                self.copy(member, self.me).wait_send()

        def total(self, parts):
            near, far = self.order[: self.near], self.order[self.near :]
            self.received(near)
            value = parts[self.me].astype(F32)
            for member in near:
                value = value + parts[member].astype(F32)
            self.received(far)
            for member in far:
                value = value + parts[member].astype(F32)
            return value

    over_t = functools.partial(Exchange, t, t_order, t_near, lambda m: (d, m))
    over_dp = functools.partial(Exchange, d, dp_order, dp_near, lambda m: (m, t))

    def block_rows(block):
        return pl.ds(pl.multiple_of(block * own_toks, own_toks), own_toks)

    def top_rows(block):
        return pl.ds(pl.multiple_of(block * own_toks, half), half)

    def low_rows(block):
        return pl.ds(pl.multiple_of(block * own_toks + half, half), half)

    def columns(j):
        return pl.ds(pl.multiple_of(j * width, width), width)

    def own_local(j):
        return pltpu.make_async_copy(g_hbm.at[:, columns(j)], g_all.at[j, block_rows(t), :], loc_sem.at[j])

    def own_to(j, which, dev):
        return remote(
            g_hbm.at[:, columns(j)], g_all.at[j, block_rows(t), :], ag_send.at[j, which], ag_recv.at[j, which], (d, dev)
        )

    def pass_on(j, which, rows, dev):
        ref = g_all.at[j, rows, :]
        return remote(ref, ref, ag_send.at[j, which], ag_recv.at[j, which], (d, dev))

    def start_own(j):
        own_to(j, 0, up).start()
        own_to(j, 1, down).start()
        own_to(j, 2, partner).start()
        own_local(j).start()

    def forward_near(j):
        pass_on(j, 0, block_rows(down), up).wait_recv()
        pass_on(j, 3, top_rows(down), up).start()
        pass_on(j, 5, block_rows(down), partner).start()
        pass_on(j, 1, block_rows(up), down).wait_recv()
        pass_on(j, 4, low_rows(up), down).start()
        pass_on(j, 6, block_rows(up), partner).start()

    def forward_far(j):
        pass_on(j, 3, top_rows(across), up).wait_recv()
        pass_on(j, 4, low_rows(across), down).wait_recv()
        pass_on(j, 7, block_rows(across), partner).start()

    def arrived(j):
        own_local(j).wait()
        pass_on(j, 2, block_rows(partner), partner).wait_recv()
        pass_on(j, 5, block_rows(other(down)), partner).wait_recv()
        pass_on(j, 6, block_rows(other(up)), partner).wait_recv()
        pass_on(j, 7, block_rows(other(across)), partner).wait_recv()

    def product(j):
        grad = mm(at_ref[:ffl, :], g_all[j])
        merged_ref[:, columns(j)] = (grad + e_ref[:, columns(j)].astype(F32)).astype(BF16)

    def serve_step(j):
        @pl.when(j + AHEAD < n_chunk)
        def _():
            start_own(j + AHEAD)

        @pl.when(j < n_chunk)
        def _():
            forward_near(j)

        @pl.when(j > 0 and j <= n_chunk if isinstance(j, int) else (j > 0) & (j <= n_chunk))
        def _():
            forward_far(j - 1)

    served = 0
    done = 0

    def serve(count):
        nonlocal served
        count = min(count, n_chunk + 1 - served)
        for j in range(served, served + count):
            serve_step(j)
        served += count

    def fill(count):
        nonlocal served, done
        count = min(count, n_chunk - done)
        lead = served - done

        def chunk(j, _):
            serve_step(j + lead)
            arrived(j)
            product(j)
            return 0

        if count > 0:
            lax.fori_loop(done, done + count, chunk, 0)
        done += count
        served = min(served + count, n_chunk + 1)

    load_b.wait()
    load_g.wait()
    gbt_all[t] = mm_nt(basis_ref[...], g_own[...]).astype(BF16)
    pl.semaphore_wait(barrier, n_t - 1 + n_dp - 1)
    x1 = over_t(lambda m: gbt_all.at[t], lambda m: gbt_all.at[m], x1s, x1r)
    x1.start()
    for j in range(min(AHEAD, n_chunk)):
        start_own(j)

    bb_ref[...] = jnp.concatenate([basis_ref[...], basis_ref[...]], axis=0).T
    padded = n_x * n_y * part
    if padded > ffl:
        at_ref[ffl:, :] = jnp.zeros((padded - ffl, toks), BF16)
        ep_ref[ffl:, :] = jnp.zeros((padded - ffl, 2 * rank), F32)

    def error_term(i, _):
        load_e(i).wait()
        rows = pl.ds(pl.multiple_of(i * step, step), step)
        ep_ref[rows, :] = mm(e_ref[rows, :], bb_ref[...])
        return 0

    lax.fori_loop(0, n_step, error_term, 0)
    load_a.wait()
    serve(SERVE["error"])

    x1.received()
    turned = jnp.concatenate([gbt_all[m] for m in range(n_t)], axis=1)
    gb_all[...] = jnp.concatenate([turned, turned], axis=0).T

    def part_rows(m):
        return pl.ds(pl.multiple_of(m * part, 16), part)

    x2 = over_dp(lambda m: p_send.at[part_rows(m), :], lambda m: p_parts.at[m], x2s, x2r)
    for dy in [*range(1, n_y), 0]:
        rows = pl.ds(pl.multiple_of(lax.rem(y + dy, n_y) * (n_x * part), 16), n_x * part)
        p_send[rows, :] = pair(mm(at_ref[rows, :], gb_all[...]) + ep_ref[rows, :])
        for dx in range(n_x):
            if dy or dx:
                x2.start_one(place(dy, dx))
    p_parts[d] = p_send[part_rows(d), :]
    serve(SERVE["left_sum"])
    fill(FILL["left_sum"])
    p_all[part_rows(d), :] = pair(fold(x2.total(p_parts)))
    x3 = over_dp(lambda m: p_all.at[part_rows(d), :], lambda m: p_all.at[part_rows(m), :], x3s, x3r)
    x3.start()
    serve(SERVE["left_rows"])
    fill(FILL["left_rows"])
    x3.received()

    pt_ref[...] = p_all[:ffl, :].T
    gram = fold(fold_rows(mm(pt_ref[...], p_all[:ffl, :])))
    lane_id = lax.broadcasted_iota(jnp.int32, (rank, 2 * rank), 1)
    row_id = lax.broadcasted_iota(jnp.int32, (rank, 2 * rank), 0)
    gram_all[t] = jnp.where(lane_id[: rank // 2] < rank, gram[: rank // 2], gram[rank // 2 :])
    x4 = over_t(lambda m: gram_all.at[t], lambda m: gram_all.at[m], x4s, x4r)
    x4.start()
    turned = pair_rows(fold_rows(mm(pt_ref[...], at_ref[:ffl, :])))
    for m in range(n_t):
        y_send[m] = turned[:, m * own_toks : (m + 1) * own_toks]
    x5 = over_t(lambda m: y_send.at[m], lambda m: y_parts.at[m], x5s, x5r)
    x5.start()
    y_parts[t] = y_send[t]

    wide = min(WIDE, d_model)

    def wide_columns(j):
        return pl.ds(pl.multiple_of(j * wide, wide), wide)

    def right_error(j, _):
        q_loc[:, wide_columns(j)] = fold_rows(mm(pt_ref[...], e_ref[:, wide_columns(j)]))
        return 0

    lax.fori_loop(0, d_model // wide, right_error, 0)
    serve(SERVE["gram"])
    fill(FILL["gram"])

    gram = x4.total(gram_all)
    gram = jnp.concatenate([gram, pltpu.roll(gram, rank, 1)], axis=0)
    elim_ref[...] = jnp.where(lane_id < rank, gram, jnp.where(lane_id - rank == row_id, 1.0, 0.0))
    group = 4

    def lane_of(x, k):
        return jnp.sum(jnp.where(lane_id[: x.shape[0]] == k, x, 0.0), axis=1, keepdims=True)

    def eliminate(i, _):
        k = i * group
        x = elim_ref[...]
        rows = [elim_ref[pl.ds(k + a, 1), :] for a in range(group)]
        cols = [lane_of(x, k + a) for a in range(group)]
        corner = [[lane_of(rows[a], k + b) for b in range(group)] for a in range(group)]
        for a in range(group):
            scale = 1.0 / corner[a][a]
            x = x - jnp.where(row_id > k + a, cols[a] * scale, 0.0) * rows[a]
            for b in range(a + 1, group):
                weight = corner[a][b] * scale
                cols[b] = cols[b] - cols[a] * weight
                rows[b] = rows[b] - rows[a] * weight
                for c in range(b, group):
                    corner[b][c] = corner[b][c] - corner[a][c] * weight
        elim_ref[...] = x
        return 0

    lax.fori_loop(0, rank // group, eliminate, 0)
    reduced = elim_ref[...]
    reduced = reduced * lax.rsqrt(lane_of_diagonal(reduced, lane_id, row_id))
    both = pair_rows(jnp.where(lane_id < rank, pltpu.roll(reduced, rank, 1), reduced))

    serve(SERVE["inverse"])

    acts = pair_rows(fold_rows(x5.total(y_parts)))

    def q_block(m):
        return (
            pl.ds(pl.multiple_of(lax.div(m, n_x) * q_rows, 16), q_rows),
            pl.ds(pl.multiple_of(lax.rem(m, n_x) * q_cols, 128), q_cols),
        )

    x6 = over_dp(lambda m: q_send.at[q_block(m)], lambda m: q_parts.at[m], x6s, x6r)
    for dx in [*range(1, n_x), 0]:
        cols = q_block(place(0, dx))[1]
        raw = q_loc[:, cols] + fold_rows(mm(acts, g_own[:, cols]))
        q_send[:, cols] = fold_rows(mm(both, pair_rows(raw))).astype(BF16)
        for dy in range(n_y):
            if dy or dx:
                x6.start_one(place(dy, dx))

    q_parts[d] = q_send[q_block(d)]
    phat_out[...] = fold(mm_nt(p_all[:ffl, :], both)).astype(BF16)
    phat_t_out[...] = fold_rows(mm(both, pt_ref[...])).astype(BF16)
    fill(FILL["right_sum"])
    q_cross[t] = x6.total(q_parts).astype(BF16)
    x7 = over_t(lambda m: q_cross.at[t], lambda m: q_cross.at[m], x7s, x7r)
    x7.start()
    fill(FILL["right_cross"])
    q = x7.total(q_cross)
    qt_out[q_block(d)] = (q / n_dp).astype(BF16)
    x8 = over_dp(lambda m: qt_out.at[q_block(d)], lambda m: qt_out.at[q_block(m)], x8s, x8r)
    x8.start()
    fill(n_chunk)

    for each in (x1, x2, x3, x4, x5, x6, x7):
        each.sent()

    def drain(j, _):
        own_to(j, 0, up).wait_send()
        own_to(j, 1, down).wait_send()
        own_to(j, 2, partner).wait_send()
        pass_on(j, 3, top_rows(down), up).wait_send()
        pass_on(j, 4, low_rows(up), down).wait_send()
        pass_on(j, 5, block_rows(down), partner).wait_send()
        pass_on(j, 6, block_rows(up), partner).wait_send()
        pass_on(j, 7, block_rows(across), partner).wait_send()
        return 0

    lax.fori_loop(0, n_chunk, drain, 0)
    x8.received()
    x8.sent()


def final_kernel(
    merged_ref, phat_ref, phat_t_ref, qt_ref, update_hbm, new_hbm, update_ref, new_ref, update_sem, new_sem
):
    rank, d_model = qt_ref.shape
    cols, ffl = update_ref.shape
    n_step = new_sem.shape[0]
    step = ffl // n_step

    def out(i):
        rows = pl.ds(pl.multiple_of(i * step, step), step)
        return pltpu.make_async_copy(new_ref.at[rows, :], new_hbm.at[0, rows, :], new_sem.at[i])

    def work(i, _):
        rows = pl.ds(pl.multiple_of(i * step, step), step)
        full = mm(phat_ref[rows, :rank], qt_ref[...])
        new_ref[rows, :] = (merged_ref[rows, :].astype(F32) - full).astype(BF16)
        out(i).start()
        return 0

    lax.fori_loop(0, n_step, work, 0)
    shift = lax.rem(d_model - lax.axis_index("dp") * cols, d_model)
    moved = pltpu.roll(qt_ref[...].astype(F32), shift, 1)
    update_ref[...] = mm_tn(moved[:, :cols].astype(BF16), phat_t_ref[...]).astype(BF16)
    update = pltpu.make_async_copy(update_ref, update_hbm, update_sem)
    update.start()

    def ended(i, _):
        out(i).wait()
        return 0

    lax.fori_loop(0, n_step, ended, 0)
    update.wait()


def shards(n_dp, n_t, acts, grads, error, basis):
    ffl, toks = acts.shape[1], acts.shape[0]
    own_toks, d_model = grads.shape
    rank = basis.shape[1]
    width = CHUNK
    n_chunk = d_model // width
    part = -(-ffl // (16 * n_dp)) * 16
    q_split = split_of(n_dp)
    q_rows, q_cols = rank // q_split[0], d_model // q_split[1]
    dma = pltpu.SemaphoreType.DMA
    anywhere = pl.BlockSpec(memory_space=pltpu.HBM)
    vmem = pl.BlockSpec(memory_space=pltpu.VMEM)
    factors = pl.pallas_call(
        functools.partial(step_kernel, n_dp, n_t, *q_split),
        out_shape=(
            pltpu.VMEM((ffl, d_model), BF16),
            pltpu.VMEM((ffl, 2 * rank), BF16),
            pltpu.VMEM((rank, ffl), BF16),
            pltpu.VMEM((rank, d_model), BF16),
        ),
        in_specs=[anywhere] * 4,
        out_specs=(vmem,) * 4,
        scratch_shapes=[
            pltpu.VMEM((n_dp * part, toks), BF16),
            pltpu.VMEM((ffl, d_model), BF16),
            pltpu.VMEM((own_toks, d_model), BF16),
            pltpu.VMEM((n_chunk, toks, width), BF16),
            pltpu.VMEM((rank, d_model), BF16),
            pltpu.VMEM((d_model, 2 * rank), BF16),
            pltpu.VMEM((n_t, rank, own_toks), BF16),
            pltpu.VMEM((toks, 2 * rank), BF16),
            pltpu.VMEM((n_dp * part, 2 * rank), F32),
            pltpu.VMEM((n_dp * part, 2 * rank), BF16),
            pltpu.VMEM((n_dp, part, 2 * rank), BF16),
            pltpu.VMEM((n_dp * part, 2 * rank), BF16),
            pltpu.VMEM((2 * rank, ffl), BF16),
            pltpu.VMEM((n_t, rank // 2, 2 * rank), F32),
            pltpu.VMEM((rank, 2 * rank), F32),
            pltpu.VMEM((n_t, 2 * rank, own_toks), BF16),
            pltpu.VMEM((n_t, 2 * rank, own_toks), BF16),
            pltpu.VMEM((rank, d_model), F32),
            pltpu.VMEM((rank, d_model), BF16),
            pltpu.VMEM((n_dp, q_rows, q_cols), BF16),
            pltpu.VMEM((n_t, q_rows, q_cols), BF16),
            dma((3,)),
            dma((pieces(ffl, 2),)),
            dma((n_chunk,)),
            dma((n_chunk, 8)),
            dma((n_chunk, 8)),
        ]
        + [dma((n,)) for n in (n_t, n_dp, n_dp, n_t, n_t, n_dp, n_t, n_dp) for _ in range(2)],
        compiler_params=pltpu.CompilerParams(
            collective_id=0, has_side_effects=True, vmem_limit_bytes=55 * 2**20
        ),
    )(acts.T, grads, error, basis.T)

    cols = d_model // n_dp
    update, new_error = pl.pallas_call(
        final_kernel,
        out_shape=(
            jax.ShapeDtypeStruct((cols, ffl), BF16),
            jax.ShapeDtypeStruct((1, ffl, d_model), BF16),
        ),
        in_specs=[vmem] * 4,
        out_specs=(anywhere,) * 2,
        scratch_shapes=[
            pltpu.VMEM((cols, ffl), BF16),
            pltpu.VMEM((ffl, d_model), BF16),
            dma,
            dma((pieces(ffl, 5),)),
        ],
        compiler_params=pltpu.CompilerParams(vmem_limit_bytes=40 * 2**20),
    )(*factors)
    return update.T, new_error


def solution(mesh):
    n_dp, n_t = mesh.shape["dp"], mesh.shape["tensor"]
    return jax.shard_map(
        functools.partial(shards, n_dp, n_t),
        mesh=mesh,
        in_specs=(P("dp", "tensor"), P(("dp", "tensor"), None), P("dp", "tensor", None), P()),
        out_specs=(P("tensor", "dp"), P("dp", "tensor", None)),
        check_vma=False,
    )
```

```python
import functools

import jax
import jax.numpy as jnp
from jax import lax
from jax.experimental import pallas as pl
from jax.experimental.pallas import tpu as pltpu
from jax.sharding import PartitionSpec as P

MESH = pl.DeviceIdType.MESH
F32 = jnp.float32
BF16 = jnp.bfloat16
CHUNK = 256
WIDE = 1280
AHEAD = 4
SERVE = {"error": 1, "left_sum": 1, "left_rows": 0, "gram": 1, "inverse": 1}
FILL = {"left_sum": 0, "left_rows": 2, "gram_dp": 0, "gram": 0, "right_sum": 2, "right_cross": 2}


def mm(a, b):
    return lax.dot_general(a, b, (((1,), (0,)), ((), ())), preferred_element_type=F32)


def mm_tn(a, b):
    return lax.dot_general(a, b, (((0,), (0,)), ((), ())), preferred_element_type=F32)


def mm_nt(a, b):
    return lax.dot_general(a, b, (((1,), (1,)), ((), ())), preferred_element_type=F32)


def fold(x):
    return x + pltpu.roll(x, x.shape[1] // 2, 1)


def fold_rows(x):
    half = x.shape[0] // 2
    return x[:half] + x[half:]


def pair(x):
    lane = lax.broadcasted_iota(jnp.int32, x.shape, 1)
    high = x.astype(BF16).astype(F32)
    return jnp.where(lane < x.shape[1] // 2, x, x - high).astype(BF16)


def pair_rows(x):
    high = x.astype(BF16)
    return jnp.concatenate([high, (x - high.astype(F32)).astype(BF16)], axis=0)


def split_of(n_dp):
    rows = 1
    while rows * rows < n_dp:
        rows *= 2
    return rows, n_dp // rows


def pieces(total, count):
    while total % (16 * count):
        count -= 1
    return count


def lane_of_diagonal(x, lane_id, row_id):
    return jnp.sum(jnp.where(lane_id == row_id, x, 0.0), axis=1, keepdims=True)


def step_kernel(
    n_dp, n_t, n_y, n_x,
    at_hbm, g_hbm, e_hbm, bt_hbm,
    merged_ref, phat_out, phat_t_out, qt_out,
    at_ref, e_ref, g_own, g_all, basis_ref, bb_ref,
    gbt_all, gb_all, ep_ref, p_send, p_parts, p_all, pt_ref, gram_all, gram_dp, elim_ref,
    y_send, y_parts, q_loc, q_send, q_parts, q_cross,
    load_sem, e_sem, loc_sem, ag_send, ag_recv,
    x1s, x1r, x2s, x2r, x3s, x3r, x4s, x4r, x5s, x5r, x6s, x6r, x7s, x7r, x8s, x8r, x9s, x9r,
):
    toks = at_ref.shape[1]
    ffl = merged_ref.shape[0]
    own_toks, d_model = g_own.shape
    n_chunk = g_all.shape[0]
    width = g_all.shape[2]
    rank = qt_out.shape[0]
    half = own_toks // 2
    part = p_parts.shape[1]
    q_rows, q_cols = q_parts.shape[1:]
    d = lax.axis_index("dp")
    t = lax.axis_index("tensor")
    y, x = lax.div(d, n_x), lax.rem(d, n_x)
    core = lax.rem(t, 2)
    partner = t + 1 - 2 * core
    up = lax.rem(t + 2, n_t)
    down = lax.rem(t + n_t - 2, n_t)
    across = lax.rem(t + 4, n_t)

    def other(block):
        return block + 1 - 2 * lax.rem(block, 2)


    barrier = pltpu.get_barrier_semaphore()

    def greet_t(k, _):
        pl.semaphore_signal(barrier, inc=1, device_id=(d, lax.rem(t + k, n_t)), device_id_type=MESH)
        return 0

    def greet_d(k, _):
        pl.semaphore_signal(barrier, inc=1, device_id=(lax.rem(d + k, n_dp), t), device_id_type=MESH)
        return 0

    lax.fori_loop(1, n_t, greet_t, 0)
    lax.fori_loop(1, n_dp, greet_d, 0)

    n_step = e_sem.shape[0]
    step = ffl // n_step
    load_g = pltpu.make_async_copy(g_hbm, g_own, load_sem.at[0])
    load_b = pltpu.make_async_copy(bt_hbm, basis_ref, load_sem.at[1])
    load_a = pltpu.make_async_copy(at_hbm, at_ref.at[:ffl, :], load_sem.at[2])
    load_g.start()
    load_b.start()

    def load_e(i):
        rows = pl.ds(pl.multiple_of(i * step, step), step)
        return pltpu.make_async_copy(e_hbm.at[0, rows, :], e_ref.at[rows, :], e_sem.at[i])

    for i in range(n_step):
        load_e(i).start()
    load_a.start()

    def remote(src, dst, ssem, rsem, dev):
        return pltpu.make_async_remote_copy(
            src_ref=src, dst_ref=dst, send_sem=ssem, recv_sem=rsem, device_id=dev, device_id_type=MESH
        )

    def place(dy, dx):
        return lax.rem(y + dy, n_y) * n_x + lax.rem(x + dx, n_x)

    def hops(dy, dx):
        return min(dy, n_y - dy) + min(dx, n_x - dx)

    offsets = [(dy, dx) for dy in range(n_y) for dx in range(n_x) if dy or dx]
    dp_order = [place(*o) for o in sorted(offsets, key=lambda o: hops(*o))]
    dp_near = sum(hops(*o) < 3 for o in offsets)
    t_order = [partner, up, down, other(up), other(down), across, other(across)]
    t_near = 5

    class Exchange:
        def __init__(self, n, me, order, near, dev, src, dst, ssem, rsem):
            self.me, self.order, self.near = me, order, near
            self.ring = [lax.rem(me + k, n) for k in range(1, n)]
            self.copy = lambda member, slot: remote(src(member), dst(slot), ssem.at[member], rsem.at[slot], dev(member))

        def start_one(self, member):
            self.copy(member, self.me).start()

        def start(self):
            for member in self.ring:
                self.start_one(member)

        def received(self, members=None):
            for member in self.order if members is None else members:
                self.copy(member, member).wait_recv()

        def sent(self):
            for member in self.order:
                self.copy(member, self.me).wait_send()

        def total(self, parts):
            near, far = self.order[: self.near], self.order[self.near :]
            self.received(near)
            value = parts[self.me].astype(F32)
            for member in near:
                value = value + parts[member].astype(F32)
            self.received(far)
            for member in far:
                value = value + parts[member].astype(F32)
            return value

    over_t = functools.partial(Exchange, n_t, t, t_order, t_near, lambda m: (d, m))
    over_dp = functools.partial(Exchange, n_dp, d, dp_order, dp_near, lambda m: (m, t))

    def block_rows(block):
        return pl.ds(pl.multiple_of(block * own_toks, own_toks), own_toks)

    def top_rows(block):
        return pl.ds(pl.multiple_of(block * own_toks, half), half)

    def low_rows(block):
        return pl.ds(pl.multiple_of(block * own_toks + half, half), half)

    def columns(j):
        return pl.ds(pl.multiple_of(j * width, width), width)

    def own_local(j):
        return pltpu.make_async_copy(g_hbm.at[:, columns(j)], g_all.at[j, block_rows(t), :], loc_sem.at[j])

    def own_to(j, which, dev):
        return remote(
            g_hbm.at[:, columns(j)], g_all.at[j, block_rows(t), :], ag_send.at[j, which], ag_recv.at[j, which], (d, dev)
        )

    def pass_on(j, which, rows, dev):
        ref = g_all.at[j, rows, :]
        return remote(ref, ref, ag_send.at[j, which], ag_recv.at[j, which], (d, dev))

    def start_own(j):
        own_to(j, 0, up).start()
        own_to(j, 1, down).start()
        own_to(j, 2, partner).start()
        own_local(j).start()

    def forward_near(j):
        pass_on(j, 0, block_rows(down), up).wait_recv()
        pass_on(j, 3, top_rows(down), up).start()
        pass_on(j, 5, block_rows(down), partner).start()
        pass_on(j, 1, block_rows(up), down).wait_recv()
        pass_on(j, 4, low_rows(up), down).start()
        pass_on(j, 6, block_rows(up), partner).start()

    def forward_far(j):
        pass_on(j, 3, top_rows(across), up).wait_recv()
        pass_on(j, 4, low_rows(across), down).wait_recv()
        pass_on(j, 7, block_rows(across), partner).start()

    def arrived(j):
        own_local(j).wait()
        pass_on(j, 2, block_rows(partner), partner).wait_recv()
        pass_on(j, 5, block_rows(other(down)), partner).wait_recv()
        pass_on(j, 6, block_rows(other(up)), partner).wait_recv()
        pass_on(j, 7, block_rows(other(across)), partner).wait_recv()

    def product(j):
        grad = mm(at_ref[:ffl, :], g_all[j])
        merged_ref[:, columns(j)] = (grad + e_ref[:, columns(j)].astype(F32)).astype(BF16)

    def serve_step(j):
        @pl.when(j + AHEAD < n_chunk)
        def _():
            start_own(j + AHEAD)

        @pl.when(j < n_chunk)
        def _():
            forward_near(j)

        @pl.when(j > 0 and j <= n_chunk if isinstance(j, int) else (j > 0) & (j <= n_chunk))
        def _():
            forward_far(j - 1)

    served = 0
    done = 0

    def serve(count):
        nonlocal served
        count = min(count, n_chunk + 1 - served)
        for j in range(served, served + count):
            serve_step(j)
        served += count

    def fill(count):
        nonlocal served, done
        count = min(count, n_chunk - done)
        lead = served - done

        def chunk(j, _):
            serve_step(j + lead)
            arrived(j)
            product(j)
            return 0

        if count > 0:
            lax.fori_loop(done, done + count, chunk, 0)
        done += count
        served = min(served + count, n_chunk + 1)

    load_b.wait()
    load_g.wait()
    gbt_all[t] = mm_nt(basis_ref[...], g_own[...]).astype(BF16)
    pl.semaphore_wait(barrier, n_t - 1 + n_dp - 1)
    x1 = over_t(lambda m: gbt_all.at[t], lambda m: gbt_all.at[m], x1s, x1r)
    x1.start()
    for j in range(min(AHEAD, n_chunk)):
        start_own(j)

    bb_ref[...] = jnp.concatenate([basis_ref[...], basis_ref[...]], axis=0).T
    padded = n_x * n_y * part
    if padded > ffl:
        at_ref[ffl:, :] = jnp.zeros((padded - ffl, toks), BF16)
        ep_ref[ffl:, :] = jnp.zeros((padded - ffl, 2 * rank), F32)

    def error_term(i, _):
        load_e(i).wait()
        rows = pl.ds(pl.multiple_of(i * step, step), step)
        ep_ref[rows, :] = mm(e_ref[rows, :], bb_ref[...])
        return 0

    lax.fori_loop(0, n_step, error_term, 0)
    load_a.wait()
    serve(SERVE["error"])

    x1.received()
    turned = jnp.concatenate([gbt_all[m] for m in range(n_t)], axis=1)
    gb_all[...] = jnp.concatenate([turned, turned], axis=0).T

    def part_rows(m):
        return pl.ds(pl.multiple_of(m * part, 16), part)

    x2 = over_dp(lambda m: p_send.at[part_rows(m), :], lambda m: p_parts.at[m], x2s, x2r)
    for dy in [*range(1, n_y), 0]:
        rows = pl.ds(pl.multiple_of(lax.rem(y + dy, n_y) * (n_x * part), 16), n_x * part)
        p_send[rows, :] = pair(mm(at_ref[rows, :], gb_all[...]) + ep_ref[rows, :])
        for dx in range(n_x):
            if dy or dx:
                x2.start_one(place(dy, dx))
    p_parts[d] = p_send[part_rows(d), :]
    serve(SERVE["left_sum"])
    fill(FILL["left_sum"])
    own = pair(fold(x2.total(p_parts)))
    p_all[part_rows(d), :] = own
    x3 = over_dp(lambda m: p_all.at[part_rows(d), :], lambda m: p_all.at[part_rows(m), :], x3s, x3r)
    x3.start()

    gram = fold(fold_rows(mm_tn(own, own)))
    lane_id = lax.broadcasted_iota(jnp.int32, (rank, 2 * rank), 1)
    row_id = lax.broadcasted_iota(jnp.int32, (rank, 2 * rank), 0)
    gram_all[t] = jnp.where(lane_id[: rank // 2] < rank, gram[: rank // 2], gram[rank // 2 :])
    x4 = over_t(lambda m: gram_all.at[t], lambda m: gram_all.at[m], x4s, x4r)
    x4.start()
    serve(SERVE["left_rows"])
    fill(FILL["left_rows"])
    gram_dp[d] = x4.total(gram_all)
    x9 = over_dp(lambda m: gram_dp.at[d], lambda m: gram_dp.at[m], x9s, x9r)
    x9.start()
    fill(FILL["gram_dp"])
    x3.received()

    pt_ref[...] = p_all[:ffl, :].T
    turned = pair_rows(fold_rows(mm(pt_ref[...], at_ref[:ffl, :])))
    for m in range(n_t):
        y_send[m] = turned[:, m * own_toks : (m + 1) * own_toks]
    x5 = over_t(lambda m: y_send.at[m], lambda m: y_parts.at[m], x5s, x5r)
    x5.start()
    y_parts[t] = y_send[t]

    wide = min(WIDE, d_model)

    def wide_columns(j):
        return pl.ds(pl.multiple_of(j * wide, wide), wide)

    def right_error(j, _):
        q_loc[:, wide_columns(j)] = fold_rows(mm(pt_ref[...], e_ref[:, wide_columns(j)]))
        return 0

    lax.fori_loop(0, d_model // wide, right_error, 0)
    serve(SERVE["gram"])
    fill(FILL["gram"])

    gram = x9.total(gram_dp)
    gram = jnp.concatenate([gram, pltpu.roll(gram, rank, 1)], axis=0)
    elim_ref[...] = jnp.where(lane_id < rank, gram, jnp.where(lane_id - rank == row_id, 1.0, 0.0))
    group = 4

    def lane_of(x, k):
        return jnp.sum(jnp.where(lane_id[: x.shape[0]] == k, x, 0.0), axis=1, keepdims=True)

    def eliminate(i, _):
        k = i * group
        x = elim_ref[...]
        rows = [elim_ref[pl.ds(k + a, 1), :] for a in range(group)]
        cols = [lane_of(x, k + a) for a in range(group)]
        corner = [[lane_of(rows[a], k + b) for b in range(group)] for a in range(group)]
        for a in range(group):
            scale = 1.0 / corner[a][a]
            x = x - jnp.where(row_id > k + a, cols[a] * scale, 0.0) * rows[a]
            for b in range(a + 1, group):
                weight = corner[a][b] * scale
                cols[b] = cols[b] - cols[a] * weight
                rows[b] = rows[b] - rows[a] * weight
                for c in range(b, group):
                    corner[b][c] = corner[b][c] - corner[a][c] * weight
        elim_ref[...] = x
        return 0

    lax.fori_loop(0, rank // group, eliminate, 0)
    reduced = elim_ref[...]
    reduced = reduced * lax.rsqrt(lane_of_diagonal(reduced, lane_id, row_id))
    both = pair_rows(jnp.where(lane_id < rank, pltpu.roll(reduced, rank, 1), reduced))

    serve(SERVE["inverse"])

    acts = pair_rows(fold_rows(x5.total(y_parts)))

    def q_block(m):
        return (
            pl.ds(pl.multiple_of(lax.div(m, n_x) * q_rows, 16), q_rows),
            pl.ds(pl.multiple_of(lax.rem(m, n_x) * q_cols, 128), q_cols),
        )

    x6 = over_dp(lambda m: q_send.at[q_block(m)], lambda m: q_parts.at[m], x6s, x6r)
    for dx in [*range(1, n_x), 0]:
        cols = q_block(place(0, dx))[1]
        raw = q_loc[:, cols] + fold_rows(mm(acts, g_own[:, cols]))
        q_send[:, cols] = fold_rows(mm(both, pair_rows(raw))).astype(BF16)
        for dy in range(n_y):
            if dy or dx:
                x6.start_one(place(dy, dx))

    q_parts[d] = q_send[q_block(d)]
    phat_out[...] = fold(mm_nt(p_all[:ffl, :], both)).astype(BF16)
    phat_t_out[...] = fold_rows(mm(both, pt_ref[...])).astype(BF16)
    fill(FILL["right_sum"])
    q_cross[t] = x6.total(q_parts).astype(BF16)
    x7 = over_t(lambda m: q_cross.at[t], lambda m: q_cross.at[m], x7s, x7r)
    x7.start()
    fill(FILL["right_cross"])
    q = x7.total(q_cross)
    qt_out[q_block(d)] = (q / n_dp).astype(BF16)
    x8 = over_dp(lambda m: qt_out.at[q_block(d)], lambda m: qt_out.at[q_block(m)], x8s, x8r)
    x8.start()
    fill(n_chunk)

    for each in (x1, x2, x3, x4, x5, x6, x7, x9):
        each.sent()

    def drain(j, _):
        own_to(j, 0, up).wait_send()
        own_to(j, 1, down).wait_send()
        own_to(j, 2, partner).wait_send()
        pass_on(j, 3, top_rows(down), up).wait_send()
        pass_on(j, 4, low_rows(up), down).wait_send()
        pass_on(j, 5, block_rows(down), partner).wait_send()
        pass_on(j, 6, block_rows(up), partner).wait_send()
        pass_on(j, 7, block_rows(across), partner).wait_send()
        return 0

    lax.fori_loop(0, n_chunk, drain, 0)
    x8.received()
    x8.sent()


def final_kernel(
    merged_ref, phat_ref, phat_t_ref, qt_ref, update_hbm, new_hbm, update_ref, new_ref, update_sem, new_sem
):
    rank, d_model = qt_ref.shape
    cols, ffl = update_ref.shape
    n_step = new_sem.shape[0]
    step = ffl // n_step

    def out(i):
        rows = pl.ds(pl.multiple_of(i * step, step), step)
        return pltpu.make_async_copy(new_ref.at[rows, :], new_hbm.at[0, rows, :], new_sem.at[i])

    def work(i, _):
        rows = pl.ds(pl.multiple_of(i * step, step), step)
        full = mm(phat_ref[rows, :rank], qt_ref[...])
        new_ref[rows, :] = (merged_ref[rows, :].astype(F32) - full).astype(BF16)
        out(i).start()
        return 0

    lax.fori_loop(0, n_step, work, 0)
    shift = lax.rem(d_model - lax.axis_index("dp") * cols, d_model)
    moved = pltpu.roll(qt_ref[...].astype(F32), shift, 1)
    update_ref[...] = mm_tn(moved[:, :cols].astype(BF16), phat_t_ref[...]).astype(BF16)
    update = pltpu.make_async_copy(update_ref, update_hbm, update_sem)
    update.start()

    def ended(i, _):
        out(i).wait()
        return 0

    lax.fori_loop(0, n_step, ended, 0)
    update.wait()


def shards(n_dp, n_t, acts, grads, error, basis):
    ffl, toks = acts.shape[1], acts.shape[0]
    own_toks, d_model = grads.shape
    rank = basis.shape[1]
    width = CHUNK
    n_chunk = d_model // width
    part = -(-ffl // (16 * n_dp)) * 16
    q_split = split_of(n_dp)
    q_rows, q_cols = rank // q_split[0], d_model // q_split[1]
    dma = pltpu.SemaphoreType.DMA
    anywhere = pl.BlockSpec(memory_space=pltpu.HBM)
    vmem = pl.BlockSpec(memory_space=pltpu.VMEM)
    factors = pl.pallas_call(
        functools.partial(step_kernel, n_dp, n_t, *q_split),
        out_shape=(
            pltpu.VMEM((ffl, d_model), BF16),
            pltpu.VMEM((ffl, 2 * rank), BF16),
            pltpu.VMEM((rank, ffl), BF16),
            pltpu.VMEM((rank, d_model), BF16),
        ),
        in_specs=[anywhere] * 4,
        out_specs=(vmem,) * 4,
        scratch_shapes=[
            pltpu.VMEM((n_dp * part, toks), BF16),
            pltpu.VMEM((ffl, d_model), BF16),
            pltpu.VMEM((own_toks, d_model), BF16),
            pltpu.VMEM((n_chunk, toks, width), BF16),
            pltpu.VMEM((rank, d_model), BF16),
            pltpu.VMEM((d_model, 2 * rank), BF16),
            pltpu.VMEM((n_t, rank, own_toks), BF16),
            pltpu.VMEM((toks, 2 * rank), BF16),
            pltpu.VMEM((n_dp * part, 2 * rank), F32),
            pltpu.VMEM((n_dp * part, 2 * rank), BF16),
            pltpu.VMEM((n_dp, part, 2 * rank), BF16),
            pltpu.VMEM((n_dp * part, 2 * rank), BF16),
            pltpu.VMEM((2 * rank, ffl), BF16),
            pltpu.VMEM((n_t, rank // 2, 2 * rank), F32),
            pltpu.VMEM((n_dp, rank // 2, 2 * rank), F32),
            pltpu.VMEM((rank, 2 * rank), F32),
            pltpu.VMEM((n_t, 2 * rank, own_toks), BF16),
            pltpu.VMEM((n_t, 2 * rank, own_toks), BF16),
            pltpu.VMEM((rank, d_model), F32),
            pltpu.VMEM((rank, d_model), BF16),
            pltpu.VMEM((n_dp, q_rows, q_cols), BF16),
            pltpu.VMEM((n_t, q_rows, q_cols), BF16),
            dma((3,)),
            dma((pieces(ffl, 2),)),
            dma((n_chunk,)),
            dma((n_chunk, 8)),
            dma((n_chunk, 8)),
        ]
        + [dma((n,)) for n in (n_t, n_dp, n_dp, n_t, n_t, n_dp, n_t, n_dp, n_dp) for _ in range(2)],
        compiler_params=pltpu.CompilerParams(
            collective_id=0, has_side_effects=True, vmem_limit_bytes=55 * 2**20
        ),
    )(acts.T, grads, error, basis.T)

    cols = d_model // n_dp
    update, new_error = pl.pallas_call(
        final_kernel,
        out_shape=(
            jax.ShapeDtypeStruct((cols, ffl), BF16),
            jax.ShapeDtypeStruct((1, ffl, d_model), BF16),
        ),
        in_specs=[vmem] * 4,
        out_specs=(anywhere,) * 2,
        scratch_shapes=[
            pltpu.VMEM((cols, ffl), BF16),
            pltpu.VMEM((ffl, d_model), BF16),
            dma,
            dma((pieces(ffl, 5),)),
        ],
        compiler_params=pltpu.CompilerParams(vmem_limit_bytes=40 * 2**20),
    )(*factors)
    return update.T, new_error


def solution(mesh):
    n_dp, n_t = mesh.shape["dp"], mesh.shape["tensor"]
    return jax.shard_map(
        functools.partial(shards, n_dp, n_t),
        mesh=mesh,
        in_specs=(P("dp", "tensor"), P(("dp", "tensor"), None), P("dp", "tensor", None), P()),
        out_specs=(P("tensor", "dp"), P("dp", "tensor", None)),
        check_vma=False,
    )
```

```python
import functools

import jax
import jax.numpy as jnp
from jax import lax
from jax.experimental import pallas as pl
from jax.experimental.pallas import tpu as pltpu
from jax.sharding import PartitionSpec as P

MESH = pl.DeviceIdType.MESH
F32 = jnp.float32
BF16 = jnp.bfloat16
CHUNK = 256
WIDE = 1280
AHEAD = 4
SERVE = {"error": 1, "left_sum": 1, "left_rows": 0, "gram": 1, "inverse": 1}
FILL = {"left_sum": 0, "left_rows": 2, "gram_dp": 0, "gram": 0, "right_sum": 2, "right_cross": 2}


def mm(a, b):
    return lax.dot_general(a, b, (((1,), (0,)), ((), ())), preferred_element_type=F32)


def mm_tn(a, b):
    return lax.dot_general(a, b, (((0,), (0,)), ((), ())), preferred_element_type=F32)


def mm_nt(a, b):
    return lax.dot_general(a, b, (((1,), (1,)), ((), ())), preferred_element_type=F32)


def fold(x):
    return x + pltpu.roll(x, x.shape[1] // 2, 1)


def fold_rows(x):
    half = x.shape[0] // 2
    return x[:half] + x[half:]


def pair(x):
    lane = lax.broadcasted_iota(jnp.int32, x.shape, 1)
    high = x.astype(BF16).astype(F32)
    return jnp.where(lane < x.shape[1] // 2, x, x - high).astype(BF16)


def pair_rows(x):
    high = x.astype(BF16)
    return jnp.concatenate([high, (x - high.astype(F32)).astype(BF16)], axis=0)


def split_of(n_dp):
    rows = 1
    while rows * rows < n_dp:
        rows *= 2
    return rows, n_dp // rows


def pieces(total, count):
    while total % (16 * count):
        count -= 1
    return count


def lane_of_diagonal(x, lane_id, row_id):
    return jnp.sum(jnp.where(lane_id == row_id, x, 0.0), axis=1, keepdims=True)


def step_kernel(
    n_dp, n_t, n_y, n_x,
    at_hbm, g_hbm, e_hbm, bt_hbm,
    merged_ref, phat_out, phat_t_out, qt_out,
    at_ref, e_ref, g_own, g_all, basis_ref, bb_ref,
    gbt_all, gb_all, ep_ref, p_send, p_parts, p_all, pt_ref, gram_all, gram_dp, elim_ref,
    y_send, y_parts, q_loc, q_send, q_parts, q_cross,
    load_sem, e_sem, loc_sem, ag_send, ag_recv,
    x1s, x1r, x2s, x2r, x3s, x3r, x4s, x4r, x5s, x5r, x6s, x6r, x7s, x7r, x8s, x8r, x9s, x9r,
):
    toks = at_ref.shape[1]
    ffl = merged_ref.shape[0]
    own_toks, d_model = g_own.shape
    n_chunk = g_all.shape[0]
    width = g_all.shape[2]
    rank = qt_out.shape[0]
    half = own_toks // 2
    part = p_parts.shape[1]
    q_rows, q_cols = q_parts.shape[1:]
    d = lax.axis_index("dp")
    t = lax.axis_index("tensor")
    y, x = lax.div(d, n_x), lax.rem(d, n_x)
    core = lax.rem(t, 2)
    partner = t + 1 - 2 * core
    up = lax.rem(t + 2, n_t)
    down = lax.rem(t + n_t - 2, n_t)
    across = lax.rem(t + 4, n_t)

    def other(block):
        return block + 1 - 2 * lax.rem(block, 2)


    barrier = pltpu.get_barrier_semaphore()

    def greet_t(k, _):
        pl.semaphore_signal(barrier, inc=1, device_id=(d, lax.rem(t + k, n_t)), device_id_type=MESH)
        return 0

    def greet_d(k, _):
        pl.semaphore_signal(barrier, inc=1, device_id=(lax.rem(d + k, n_dp), t), device_id_type=MESH)
        return 0

    lax.fori_loop(1, n_t, greet_t, 0)
    lax.fori_loop(1, n_dp, greet_d, 0)

    n_step = e_sem.shape[0]
    step = ffl // n_step
    load_g = pltpu.make_async_copy(g_hbm, g_own, load_sem.at[0])
    load_b = pltpu.make_async_copy(bt_hbm, basis_ref, load_sem.at[1])
    load_a = pltpu.make_async_copy(at_hbm, at_ref.at[:ffl, :], load_sem.at[2])
    load_g.start()
    load_b.start()

    def load_e(i):
        rows = pl.ds(pl.multiple_of(i * step, step), step)
        return pltpu.make_async_copy(e_hbm.at[0, rows, :], e_ref.at[rows, :], e_sem.at[i])

    for i in range(n_step):
        load_e(i).start()
    load_a.start()

    def remote(src, dst, ssem, rsem, dev):
        return pltpu.make_async_remote_copy(
            src_ref=src, dst_ref=dst, send_sem=ssem, recv_sem=rsem, device_id=dev, device_id_type=MESH
        )

    def place(dy, dx):
        return lax.rem(y + dy, n_y) * n_x + lax.rem(x + dx, n_x)

    def hops(dy, dx):
        return min(dy, n_y - dy) + min(dx, n_x - dx)

    offsets = [(dy, dx) for dy in range(n_y) for dx in range(n_x) if dy or dx]
    dp_order = [place(*o) for o in sorted(offsets, key=lambda o: hops(*o))]
    dp_near = sum(hops(*o) < 3 for o in offsets)
    t_order = [partner, up, down, other(up), other(down), across, other(across)]
    t_near = 5

    class Exchange:
        def __init__(self, n, me, order, near, dev, src, dst, ssem, rsem):
            self.me, self.order, self.near = me, order, near
            self.ring = [lax.rem(me + k, n) for k in range(1, n)]
            self.copy = lambda member, slot: remote(src(member), dst(slot), ssem.at[member], rsem.at[slot], dev(member))

        def start_one(self, member):
            self.copy(member, self.me).start()

        def start(self):
            for member in self.ring:
                self.start_one(member)

        def received(self, members=None):
            for member in self.order if members is None else members:
                self.copy(member, member).wait_recv()

        def sent(self):
            for member in self.order:
                self.copy(member, self.me).wait_send()

        def total(self, parts):
            near, far = self.order[: self.near], self.order[self.near :]
            self.received(near)
            value = parts[self.me].astype(F32)
            for member in near:
                value = value + parts[member].astype(F32)
            self.received(far)
            for member in far:
                value = value + parts[member].astype(F32)
            return value

    over_t = functools.partial(Exchange, n_t, t, t_order, t_near, lambda m: (d, m))
    over_dp = functools.partial(Exchange, n_dp, d, dp_order, dp_near, lambda m: (m, t))

    def block_rows(block):
        return pl.ds(pl.multiple_of(block * own_toks, own_toks), own_toks)

    def top_rows(block):
        return pl.ds(pl.multiple_of(block * own_toks, half), half)

    def low_rows(block):
        return pl.ds(pl.multiple_of(block * own_toks + half, half), half)

    def columns(j):
        return pl.ds(pl.multiple_of(j * width, width), width)

    def own_local(j):
        return pltpu.make_async_copy(g_hbm.at[:, columns(j)], g_all.at[j, block_rows(t), :], loc_sem.at[j])

    def own_to(j, which, dev):
        return remote(
            g_hbm.at[:, columns(j)], g_all.at[j, block_rows(t), :], ag_send.at[j, which], ag_recv.at[j, which], (d, dev)
        )

    def pass_on(j, which, rows, dev):
        ref = g_all.at[j, rows, :]
        return remote(ref, ref, ag_send.at[j, which], ag_recv.at[j, which], (d, dev))

    def start_own(j):
        own_to(j, 0, up).start()
        own_to(j, 1, down).start()
        own_to(j, 2, partner).start()
        own_local(j).start()

    def forward_near(j):
        pass_on(j, 0, block_rows(down), up).wait_recv()
        pass_on(j, 3, top_rows(down), up).start()
        pass_on(j, 5, block_rows(down), partner).start()
        pass_on(j, 1, block_rows(up), down).wait_recv()
        pass_on(j, 4, low_rows(up), down).start()
        pass_on(j, 6, block_rows(up), partner).start()

    def forward_far(j):
        pass_on(j, 3, top_rows(across), up).wait_recv()
        pass_on(j, 4, low_rows(across), down).wait_recv()
        pass_on(j, 7, block_rows(across), partner).start()

    def arrived(j):
        own_local(j).wait()
        pass_on(j, 2, block_rows(partner), partner).wait_recv()
        pass_on(j, 5, block_rows(other(down)), partner).wait_recv()
        pass_on(j, 6, block_rows(other(up)), partner).wait_recv()
        pass_on(j, 7, block_rows(other(across)), partner).wait_recv()

    def product(j):
        grad = mm(at_ref[:ffl, :], g_all[j])
        merged_ref[:, columns(j)] = (grad + e_ref[:, columns(j)].astype(F32)).astype(BF16)

    def serve_step(j):
        @pl.when(j + AHEAD < n_chunk)
        def _():
            start_own(j + AHEAD)

        @pl.when(j < n_chunk)
        def _():
            forward_near(j)

        @pl.when(j > 0 and j <= n_chunk if isinstance(j, int) else (j > 0) & (j <= n_chunk))
        def _():
            forward_far(j - 1)

    served = 0
    done = 0

    def serve(count):
        nonlocal served
        count = min(count, n_chunk + 1 - served)
        for j in range(served, served + count):
            serve_step(j)
        served += count

    def fill(count):
        nonlocal served, done
        count = min(count, n_chunk - done)
        lead = served - done

        def chunk(j, _):
            serve_step(j + lead)
            arrived(j)
            product(j)
            return 0

        if count > 0:
            lax.fori_loop(done, done + count, chunk, 0)
        done += count
        served = min(served + count, n_chunk + 1)

    load_b.wait()
    load_g.wait()
    gbt_all[t] = mm_nt(basis_ref[...], g_own[...]).astype(BF16)
    pl.semaphore_wait(barrier, n_t - 1 + n_dp - 1)
    x1 = over_t(lambda m: gbt_all.at[t], lambda m: gbt_all.at[m], x1s, x1r)
    x1.start()
    for j in range(min(AHEAD, n_chunk)):
        start_own(j)

    bb_ref[...] = jnp.concatenate([basis_ref[...], basis_ref[...]], axis=0).T
    padded = n_x * n_y * part
    if padded > ffl:
        at_ref[ffl:, :] = jnp.zeros((padded - ffl, toks), BF16)
        ep_ref[ffl:, :] = jnp.zeros((padded - ffl, 2 * rank), F32)

    def error_term(i, _):
        load_e(i).wait()
        rows = pl.ds(pl.multiple_of(i * step, step), step)
        ep_ref[rows, :] = mm(e_ref[rows, :], bb_ref[...])
        return 0

    lax.fori_loop(0, n_step, error_term, 0)
    load_a.wait()
    serve(SERVE["error"])

    x1.received()
    turned = jnp.concatenate([gbt_all[m] for m in range(n_t)], axis=1)
    gb_all[...] = jnp.concatenate([turned, turned], axis=0).T

    def part_rows(m):
        return pl.ds(pl.multiple_of(m * part, 16), part)

    x2 = over_dp(lambda m: p_send.at[part_rows(m), :], lambda m: p_parts.at[m], x2s, x2r)
    for dy in [*range(1, n_y), 0]:
        rows = pl.ds(pl.multiple_of(lax.rem(y + dy, n_y) * (n_x * part), 16), n_x * part)
        p_send[rows, :] = pair(mm(at_ref[rows, :], gb_all[...]) + ep_ref[rows, :])
        for dx in range(n_x):
            if dy or dx:
                x2.start_one(place(dy, dx))
    p_parts[d] = p_send[part_rows(d), :]
    serve(SERVE["left_sum"])
    fill(FILL["left_sum"])
    own = pair(fold(x2.total(p_parts)))
    p_all[part_rows(d), :] = own
    x3 = over_dp(lambda m: p_all.at[part_rows(d), :], lambda m: p_all.at[part_rows(m), :], x3s, x3r)
    x3.start()

    gram = fold(fold_rows(mm_tn(own, own)))
    lane_id = lax.broadcasted_iota(jnp.int32, (rank, 2 * rank), 1)
    row_id = lax.broadcasted_iota(jnp.int32, (rank, 2 * rank), 0)
    gram_all[t] = jnp.where(lane_id[: rank // 2] < rank, gram[: rank // 2], gram[rank // 2 :])
    x4 = over_t(lambda m: gram_all.at[t], lambda m: gram_all.at[m], x4s, x4r)
    x4.start()
    serve(SERVE["left_rows"])
    fill(FILL["left_rows"])
    gram_dp[d] = x4.total(gram_all)
    x9 = over_dp(lambda m: gram_dp.at[d], lambda m: gram_dp.at[m], x9s, x9r)
    x9.start()
    fill(FILL["gram_dp"])
    x3.received()

    pt_ref[...] = p_all[:ffl, :].T
    turned = pair_rows(fold_rows(mm(pt_ref[...], at_ref[:ffl, :])))
    for m in range(n_t):
        y_send[m] = turned[:, m * own_toks : (m + 1) * own_toks]
    x5 = over_t(lambda m: y_send.at[m], lambda m: y_parts.at[m], x5s, x5r)
    x5.start()
    y_parts[t] = y_send[t]

    wide = min(WIDE, d_model)

    def wide_columns(j):
        return pl.ds(pl.multiple_of(j * wide, wide), wide)

    def right_error(j, _):
        q_loc[:, wide_columns(j)] = fold_rows(mm(pt_ref[...], e_ref[:, wide_columns(j)]))
        return 0

    lax.fori_loop(0, d_model // wide, right_error, 0)
    serve(SERVE["gram"])
    fill(FILL["gram"])

    gram = x9.total(gram_dp)
    gram = jnp.concatenate([gram, pltpu.roll(gram, rank, 1)], axis=0)
    elim_ref[...] = jnp.where(lane_id < rank, gram, jnp.where(lane_id - rank == row_id, 1.0, 0.0))
    group = 4

    def lane_of(x, k):
        return jnp.sum(jnp.where(lane_id[: x.shape[0]] == k, x, 0.0), axis=1, keepdims=True)

    def eliminate(i, _):
        k = i * group
        x = elim_ref[...]
        rows = [elim_ref[pl.ds(k + a, 1), :] for a in range(group)]
        cols = [lane_of(x, k + a) for a in range(group)]
        corner = [[lane_of(rows[a], k + b) for b in range(group)] for a in range(group)]
        for a in range(group):
            scale = 1.0 / corner[a][a]
            x = x - jnp.where(row_id > k + a, cols[a] * scale, 0.0) * rows[a]
            for b in range(a + 1, group):
                weight = corner[a][b] * scale
                cols[b] = cols[b] - cols[a] * weight
                rows[b] = rows[b] - rows[a] * weight
                for c in range(b, group):
                    corner[b][c] = corner[b][c] - corner[a][c] * weight
        elim_ref[...] = x
        return 0

    lax.fori_loop(0, rank // group, eliminate, 0)
    reduced = elim_ref[...]
    reduced = reduced * lax.rsqrt(lane_of_diagonal(reduced, lane_id, row_id))
    both = pair_rows(jnp.where(lane_id < rank, pltpu.roll(reduced, rank, 1), reduced))

    serve(SERVE["inverse"])

    acts = pair_rows(fold_rows(x5.total(y_parts)))

    def q_block(m):
        return (
            pl.ds(pl.multiple_of(lax.div(m, n_x) * q_rows, 16), q_rows),
            pl.ds(pl.multiple_of(lax.rem(m, n_x) * q_cols, 128), q_cols),
        )

    x6 = over_dp(lambda m: q_send.at[q_block(m)], lambda m: q_parts.at[m], x6s, x6r)
    for dx in [*range(1, n_x), 0]:
        cols = q_block(place(0, dx))[1]
        raw = q_loc[:, cols] + fold_rows(mm(acts, g_own[:, cols]))
        q_send[:, cols] = fold_rows(mm(both, pair_rows(raw))).astype(BF16)
        for dy in range(n_y):
            if dy or dx:
                x6.start_one(place(dy, dx))

    q_parts[d] = q_send[q_block(d)]
    phat_out[...] = fold(mm_nt(p_all[:ffl, :], both)).astype(BF16)
    phat_t_out[...] = fold_rows(mm(both, pt_ref[...])).astype(BF16)
    fill(FILL["right_sum"])
    q_cross[t] = x6.total(q_parts).astype(BF16)
    x7 = over_t(lambda m: q_cross.at[t], lambda m: q_cross.at[m], x7s, x7r)
    x7.start()
    fill(FILL["right_cross"])
    for each in (x1, x2, x3, x4, x5, x9):
        each.sent()
    q = x7.total(q_cross)
    qt_out[q_block(d)] = (q / n_dp).astype(BF16)
    x8 = over_dp(lambda m: qt_out.at[q_block(d)], lambda m: qt_out.at[q_block(m)], x8s, x8r)
    x8.start()
    fill(n_chunk)

    for each in (x6, x7):
        each.sent()

    def drain(j, _):
        own_to(j, 0, up).wait_send()
        own_to(j, 1, down).wait_send()
        own_to(j, 2, partner).wait_send()
        pass_on(j, 3, top_rows(down), up).wait_send()
        pass_on(j, 4, low_rows(up), down).wait_send()
        pass_on(j, 5, block_rows(down), partner).wait_send()
        pass_on(j, 6, block_rows(up), partner).wait_send()
        pass_on(j, 7, block_rows(across), partner).wait_send()
        return 0

    lax.fori_loop(0, n_chunk, drain, 0)
    x8.received()
    x8.sent()


def final_kernel(
    merged_ref, phat_ref, phat_t_ref, qt_ref, update_hbm, new_hbm, update_ref, new_ref, update_sem, new_sem
):
    rank, d_model = qt_ref.shape
    cols, ffl = update_ref.shape
    n_step = new_sem.shape[0]
    step = ffl // n_step

    def out(i):
        rows = pl.ds(pl.multiple_of(i * step, step), step)
        return pltpu.make_async_copy(new_ref.at[rows, :], new_hbm.at[0, rows, :], new_sem.at[i])

    def work(i, _):
        rows = pl.ds(pl.multiple_of(i * step, step), step)
        full = mm(phat_ref[rows, :rank], qt_ref[...])
        new_ref[rows, :] = (merged_ref[rows, :].astype(F32) - full).astype(BF16)
        out(i).start()
        return 0

    lax.fori_loop(0, n_step, work, 0)
    shift = lax.rem(d_model - lax.axis_index("dp") * cols, d_model)
    moved = pltpu.roll(qt_ref[...].astype(F32), shift, 1)
    update_ref[...] = mm_tn(moved[:, :cols].astype(BF16), phat_t_ref[...]).astype(BF16)
    update = pltpu.make_async_copy(update_ref, update_hbm, update_sem)
    update.start()

    def ended(i, _):
        out(i).wait()
        return 0

    lax.fori_loop(0, n_step, ended, 0)
    update.wait()


def shards(n_dp, n_t, acts, grads, error, basis):
    ffl, toks = acts.shape[1], acts.shape[0]
    own_toks, d_model = grads.shape
    rank = basis.shape[1]
    width = CHUNK
    n_chunk = d_model // width
    part = -(-ffl // (16 * n_dp)) * 16
    q_split = split_of(n_dp)
    q_rows, q_cols = rank // q_split[0], d_model // q_split[1]
    dma = pltpu.SemaphoreType.DMA
    anywhere = pl.BlockSpec(memory_space=pltpu.HBM)
    vmem = pl.BlockSpec(memory_space=pltpu.VMEM)
    factors = pl.pallas_call(
        functools.partial(step_kernel, n_dp, n_t, *q_split),
        out_shape=(
            pltpu.VMEM((ffl, d_model), BF16),
            pltpu.VMEM((ffl, 2 * rank), BF16),
            pltpu.VMEM((rank, ffl), BF16),
            pltpu.VMEM((rank, d_model), BF16),
        ),
        in_specs=[anywhere] * 4,
        out_specs=(vmem,) * 4,
        scratch_shapes=[
            pltpu.VMEM((n_dp * part, toks), BF16),
            pltpu.VMEM((ffl, d_model), BF16),
            pltpu.VMEM((own_toks, d_model), BF16),
            pltpu.VMEM((n_chunk, toks, width), BF16),
            pltpu.VMEM((rank, d_model), BF16),
            pltpu.VMEM((d_model, 2 * rank), BF16),
            pltpu.VMEM((n_t, rank, own_toks), BF16),
            pltpu.VMEM((toks, 2 * rank), BF16),
            pltpu.VMEM((n_dp * part, 2 * rank), F32),
            pltpu.VMEM((n_dp * part, 2 * rank), BF16),
            pltpu.VMEM((n_dp, part, 2 * rank), BF16),
            pltpu.VMEM((n_dp * part, 2 * rank), BF16),
            pltpu.VMEM((2 * rank, ffl), BF16),
            pltpu.VMEM((n_t, rank // 2, 2 * rank), F32),
            pltpu.VMEM((n_dp, rank // 2, 2 * rank), F32),
            pltpu.VMEM((rank, 2 * rank), F32),
            pltpu.VMEM((n_t, 2 * rank, own_toks), BF16),
            pltpu.VMEM((n_t, 2 * rank, own_toks), BF16),
            pltpu.VMEM((rank, d_model), F32),
            pltpu.VMEM((rank, d_model), BF16),
            pltpu.VMEM((n_dp, q_rows, q_cols), BF16),
            pltpu.VMEM((n_t, q_rows, q_cols), BF16),
            dma((3,)),
            dma((pieces(ffl, 2),)),
            dma((n_chunk,)),
            dma((n_chunk, 8)),
            dma((n_chunk, 8)),
        ]
        + [dma((n,)) for n in (n_t, n_dp, n_dp, n_t, n_t, n_dp, n_t, n_dp, n_dp) for _ in range(2)],
        compiler_params=pltpu.CompilerParams(
            collective_id=0, has_side_effects=True, vmem_limit_bytes=55 * 2**20
        ),
    )(acts.T, grads, error, basis.T)

    cols = d_model // n_dp
    update, new_error = pl.pallas_call(
        final_kernel,
        out_shape=(
            jax.ShapeDtypeStruct((cols, ffl), BF16),
            jax.ShapeDtypeStruct((1, ffl, d_model), BF16),
        ),
        in_specs=[vmem] * 4,
        out_specs=(anywhere,) * 2,
        scratch_shapes=[
            pltpu.VMEM((cols, ffl), BF16),
            pltpu.VMEM((ffl, d_model), BF16),
            dma,
            dma((pieces(ffl, 5),)),
        ],
        compiler_params=pltpu.CompilerParams(vmem_limit_bytes=40 * 2**20),
    )(*factors)
    return update.T, new_error


def solution(mesh):
    n_dp, n_t = mesh.shape["dp"], mesh.shape["tensor"]
    return jax.shard_map(
        functools.partial(shards, n_dp, n_t),
        mesh=mesh,
        in_specs=(P("dp", "tensor"), P(("dp", "tensor"), None), P("dp", "tensor", None), P()),
        out_specs=(P("tensor", "dp"), P("dp", "tensor", None)),
        check_vma=False,
    )
```
